256 devices in a mesh: len: 32 (over z_lo, y, core), wid: 8 (over x, z_hi).
Axes of the slice: x: 4, y: 4, z: 8 (z_hi: 2, z_lo: 4; z = z_hi * 4 + z_lo), core: 2. Of those that a mesh axis runs over, the one named last changes fastest.
Arguments:
- conserved: float32 [9, 6, 6, 6, 32, 1024], P(None, None, None, None, 'len', 'wid'), may hold values from -1.3 to 12.5, as said below
- ends_kind: int32 [2, 32, 32], P(None, 'wid'), may hold values from 0 to 2
- sides_kind: int32 [2, 32, 32], P(None, 'len'), may hold values from 0 to 2
- walls_kind: int32 [2, 32, 32], P(None, 'len', 'wid'), may hold values from 0 to 2
Outputs:
- updated: float32 [9, 6, 6, 6, 32, 1024], P(None, None, None, None, 'len', 'wid')
- time_step: float32 [], replicated
The draws below stay inside these ranges and needn't reach their ends.
Inputs may be any that keep to these rules, and one draw needn't show every extreme that they name: `conserved`: density and pressure of every node lie between 0.7 and 1.4. `ends_kind`: 0 marks an inflow port of the nozzle, 1 a wall, 2 the free surface. `sides_kind`: 0 marks an inflow port of the nozzle, 1 a wall, 2 the free surface. `walls_kind`: 0 marks an inflow port of the nozzle, 1 a wall, 2 the free surface.
All inputs are finite; a program needn't handle non-finite values.
Results may differ from the reference program's by a relative error of at most 0.00012.
Values sent between devices are 32-bit elements; how exact they have to be, the bound alone decides.
A program may use at most 128 MiB of HBM per device.

```python
import math
import jax
import jax.numpy as jnp
import numpy as np
from jax import lax

EZ = 32
NXE = 32
NYE = 32


GAMMA = 5.0 / 3.0


def draw_conserved(key, part):
    key = jax.random.fold_in(key, 11)
    subkeys = jax.random.split(key, 6)
    grid_shape = (6, 6, 6, NXE, NYE * EZ)
    length_pos = (jnp.arange(NXE).astype(jnp.float32) + 0.5) / NXE
    width_pos = ((jnp.arange(NYE * EZ) // EZ).astype(jnp.float32) + 0.5) / NYE
    background = 0.5 * (1.0 + 2.0 * length_pos[:, None]) * (1.0 + width_pos[None, :])
    density = jnp.exp(jax.random.uniform(subkeys[0], grid_shape, jnp.float32, math.log(0.7), math.log(1.4)))
    pressure = jnp.exp(jax.random.uniform(subkeys[1], grid_shape, jnp.float32, math.log(0.7), math.log(1.4)))
    velocity = 0.3 * jax.random.truncated_normal(subkeys[2], -3.0, 3.0, (3,) + grid_shape, jnp.float32)
    magnetic_field = 0.3 * jax.random.truncated_normal(subkeys[3], -3.0, 3.0, (3,) + grid_shape, jnp.float32)
    cleaning = 0.2 * jax.random.truncated_normal(subkeys[4], -3.0, 3.0, grid_shape, jnp.float32)
    field_thick = magnetic_field[2] + background
    momentum = density[None] * velocity
    energy = pressure / (GAMMA - 1.0) + 0.5 * density * (velocity[0] ** 2 + velocity[1] ** 2 + velocity[2] ** 2)
    energy = energy + 0.5 * (magnetic_field[0] ** 2 + magnetic_field[1] ** 2 + field_thick ** 2) + 0.5 * cleaning ** 2
    stacked = jnp.concatenate([density[None], momentum, energy[None], magnetic_field[0][None], magnetic_field[1][None], field_thick[None], cleaning[None]], axis=0)
    return stacked.astype(jnp.float32)


def set_ends(values, key, least, top_value):
    place = [jax.random.randint(jax.random.fold_in(key, axis), (), 0, length) for axis, length in enumerate(values.shape)]
    longest = values.shape.index(max(values.shape))
    beside = place[:longest] + [(place[longest] + 1) % values.shape[longest]] + place[longest + 1:]
    return values.at[tuple(place)].set(least).at[tuple(beside)].set(top_value)


def setup_inputs(seed: int = 0) -> dict:
    key_of = jax.random.split(jax.random.key(seed), 5)
    conserved = draw_conserved(jax.random.fold_in(key_of[4], 71), 0)
    ends_kind = set_ends(jax.random.randint(key_of[1], (2, NYE, EZ), 0, 3), jax.random.fold_in(key_of[1], 1), 0, 2).astype(jnp.int32)
    sides_kind = set_ends(jax.random.randint(key_of[2], (2, NXE, EZ), 0, 3), jax.random.fold_in(key_of[2], 1), 0, 2).astype(jnp.int32)
    walls_kind = set_ends(jax.random.randint(key_of[3], (2, NXE, NYE), 0, 3), jax.random.fold_in(key_of[3], 1), 0, 2).astype(jnp.int32)
    return dict(conserved=conserved, ends_kind=ends_kind, sides_kind=sides_kind, walls_kind=walls_kind)


GAMMA = 5.0 / 3.0
GLM_SPEED = 2.0
JET_SPEED = 0.8
BRAKE_FIELD = 1.0
CFL_NUMBER = 0.1
END_WEIGHT = 1.0 / 15.0
JACOBIAN_INV = 2.0

def lgl_derivative():
    points = np.array([-1.0, -0.7650553239294647, -0.2852315164806451, 0.2852315164806451, 0.7650553239294647, 1.0])
    node_count = points.shape[0]
    barycentric = np.ones(node_count)
    for row_index in range(node_count):
        for column in range(node_count):
            if row_index != column:
                barycentric[row_index] = barycentric[row_index] / (points[row_index] - points[column])
    matrix = np.zeros((node_count, node_count))
    for row_index in range(node_count):
        for column in range(node_count):
            if row_index != column:
                matrix[row_index, column] = barycentric[column] / barycentric[row_index] / (points[row_index] - points[column])
    for row_index in range(node_count):
        matrix[row_index, row_index] = -np.sum(matrix[row_index])
    return matrix.astype(np.float32)

def take_range(array, axis_num, start, stop):
    return lax.slice_in_dim(array, start, stop, axis=axis_num)

def primitives(conserved):
    density = conserved[0]
    velocity = [conserved[1] / density, conserved[2] / density, conserved[3] / density]
    magnetic_field = [conserved[5], conserved[6], conserved[7]]
    cleaning = conserved[8]
    kinetic = 0.5 * (conserved[1] * velocity[0] + conserved[2] * velocity[1] + conserved[3] * velocity[2])
    magnetic = 0.5 * (magnetic_field[0] ** 2 + magnetic_field[1] ** 2 + magnetic_field[2] ** 2)
    pressure = (GAMMA - 1.0) * (conserved[4] - kinetic - magnetic - 0.5 * cleaning * cleaning)
    return (density, velocity, magnetic_field, cleaning, pressure, magnetic)

def directional_flux(conserved, direction):
    density, velocity, magnetic_field, cleaning, pressure, magnetic = primitives(conserved)
    total_pressure = pressure + magnetic
    normal_velocity = velocity[direction]
    normal_field = magnetic_field[direction]
    velocity_dot_field = velocity[0] * magnetic_field[0] + velocity[1] * magnetic_field[1] + velocity[2] * magnetic_field[2]
    entries = [conserved[1 + direction]]
    for component in range(3):
        momentum = conserved[1 + component] * normal_velocity - magnetic_field[component] * normal_field
        if component == direction:
            momentum = momentum + total_pressure
        entries.append(momentum)
    entries.append(normal_velocity * (conserved[4] + total_pressure) - normal_field * velocity_dot_field + GLM_SPEED * cleaning * normal_field)
    for component in range(3):
        if component == direction:
            entries.append(GLM_SPEED * cleaning)
        else:
            entries.append(normal_velocity * magnetic_field[component] - normal_field * velocity[component])
    entries.append(GLM_SPEED * normal_field)
    return jnp.stack(entries)

def wave_speed(conserved, direction):
    density, velocity, magnetic_field, cleaning, pressure, magnetic = primitives(conserved)
    acoustic_speed_sq = GAMMA * pressure / density
    along_sq = magnetic_field[direction] ** 2 / density
    transverse_axis = magnetic_field[(direction + 1) % 3] ** 2 + magnetic_field[(direction + 2) % 3] ** 2
    transverse_axis = transverse_axis / density
    alfven_speed_sq = along_sq + transverse_axis
    quadratic_discrim = (acoustic_speed_sq - alfven_speed_sq) ** 2 + 4.0 * acoustic_speed_sq * transverse_axis
    fast_magnetosonic = jnp.sqrt(0.5 * (acoustic_speed_sq + alfven_speed_sq + jnp.sqrt(quadratic_discrim)))
    return jnp.maximum(jnp.abs(velocity[direction]) + fast_magnetosonic, GLM_SPEED)

def face_kind(face_kinds, direction, side):
    if direction == 0:
        return face_kinds[0][side][None, None, None, None, :, :]
    if direction == 1:
        return face_kinds[1][side][None, None, None, :, None, :]
    return face_kinds[2][side][None, None, None, :, :, None]

def boundary_state(interior, kind_values, direction, outward):
    inflow_values = [1.0, 0.0, 0.0, 0.0, 1.0 / (GAMMA - 1.0) + 0.5 * JET_SPEED ** 2 + 0.5 * BRAKE_FIELD ** 2, 0.0, 0.0, BRAKE_FIELD, 0.0]
    inflow_values[1 + direction] = -outward * JET_SPEED
    inflow = jnp.asarray(np.array(inflow_values, dtype=np.float32)).astype(interior.dtype).reshape((9, 1, 1, 1, 1, 1))
    mirror_values = np.ones(9, dtype=np.float32)
    mirror_values[1 + direction] = -1.0
    mirror = jnp.asarray(mirror_values).astype(interior.dtype).reshape((9, 1, 1, 1, 1, 1))
    wall_state = interior * mirror
    return jnp.where(kind_values == 0, inflow, jnp.where(kind_values == 1, wall_state, interior))

def triplet(ghost_state, direction):
    return (ghost_state, directional_flux(ghost_state, direction), wave_speed(ghost_state, direction)[None])

def local_lax_friedrichs(left_state, left_flux, left_speed, right_state, right_flux, right_speed):
    return 0.5 * (left_flux + right_flux) - 0.5 * jnp.maximum(left_speed, right_speed) * (right_state - left_state)

def face_terms(accumulated, faces, ghost_low, ghost_high, direction):
    low_state, high_state, low_flux, high_flux, low_speed, high_speed = faces
    axis_elem = 3 + direction
    elem_count = low_state.shape[axis_elem]
    left_state = jnp.concatenate([ghost_low[0], high_state], axis=axis_elem)
    left_flux = jnp.concatenate([ghost_low[1], high_flux], axis=axis_elem)
    left_speed = jnp.concatenate([ghost_low[2], high_speed], axis=axis_elem)
    right_state = jnp.concatenate([low_state, ghost_high[0]], axis=axis_elem)
    right_flux = jnp.concatenate([low_flux, ghost_high[1]], axis=axis_elem)
    right_speed = jnp.concatenate([low_speed, ghost_high[2]], axis=axis_elem)
    interface = local_lax_friedrichs(left_state, left_flux, left_speed, right_state, right_flux, right_speed)
    interface_low = take_range(interface, axis_elem, 0, elem_count)
    interface_high = take_range(interface, axis_elem, 1, elem_count + 1)
    low_index = (slice(None),) * (1 + direction) + (0,)
    high_index = (slice(None),) * (1 + direction) + (5,)
    accumulated = accumulated.at[high_index].add((interface_high - high_flux) / END_WEIGHT)
    accumulated = accumulated.at[low_index].add((low_flux - interface_low) / END_WEIGHT)
    return accumulated

def operator(conserved, derivative, face_kinds):
    length_elems = conserved.shape[4]
    width_elems = conserved.shape[5] // EZ
    grid_shape = (9, 6, 6, 6, length_elems, width_elems, EZ)
    precise = lax.Precision.HIGHEST
    fluxes = [directional_flux(conserved, direction) for direction in range(3)]
    divergence = jnp.einsum('ai,vijkxm->vajkxm', derivative, fluxes[0], precision=precise)
    divergence = divergence + jnp.einsum('aj,vijkxm->viakxm', derivative, fluxes[1], precision=precise)
    divergence = divergence + jnp.einsum('ak,vijkxm->vijaxm', derivative, fluxes[2], precision=precise)
    accumulated = divergence.reshape(grid_shape)
    grid_state = conserved.reshape(grid_shape)
    for direction in range(3):
        grid_flux = fluxes[direction].reshape(grid_shape)
        low_index = (slice(None),) * (1 + direction) + (0,)
        high_index = (slice(None),) * (1 + direction) + (5,)
        low_state = grid_state[low_index]
        high_state = grid_state[high_index]
        low_flux = grid_flux[low_index]
        high_flux = grid_flux[high_index]
        low_speed = wave_speed(low_state, direction)[None]
        high_speed = wave_speed(high_state, direction)[None]
        axis_elem = 3 + direction
        elem_count = low_state.shape[axis_elem]
        outer_low = boundary_state(take_range(low_state, axis_elem, 0, 1), face_kind(face_kinds, direction, 0), direction, -1.0)
        outer_high = boundary_state(take_range(high_state, axis_elem, elem_count - 1, elem_count), face_kind(face_kinds, direction, 1), direction, 1.0)
        faces = (low_state, high_state, low_flux, high_flux, low_speed, high_speed)
        accumulated = face_terms(accumulated, faces, triplet(outer_low, direction), triplet(outer_high, direction), direction)
    return (-JACOBIAN_INV * accumulated).reshape(conserved.shape)

def reference(conserved, ends_kind, sides_kind, walls_kind):
    derivative = jnp.asarray(lgl_derivative())
    face_kinds = (ends_kind, sides_kind, walls_kind)
    fastest = jnp.max(jnp.stack([jnp.max(wave_speed(conserved, direction)) for direction in range(3)]))
    time_step = CFL_NUMBER / (11.0 * fastest)
    first_section = conserved + time_step * operator(conserved, derivative, face_kinds)
    second_section = 0.75 * conserved + 0.25 * (first_section + time_step * operator(first_section, derivative, face_kinds))
    updated = conserved / 3.0 + 2.0 / 3.0 * (second_section + time_step * operator(second_section, derivative, face_kinds))
    return (updated, time_step)
```

```python
import functools

import jax
import jax.numpy as jnp
import numpy as np
from jax import lax
from jax.experimental import pallas as pl
from jax.experimental.pallas import tpu as pltpu
from jax.sharding import PartitionSpec as P

MESH = pl.DeviceIdType.MESH

EZ = 32
LANES = 128
NODES = 216
PADDED = 224
FACE = 36
HALO = 40
PACK = 9

GAMMA = 5.0 / 3.0
GLM_SPEED = 2.0
JET_SPEED = 0.8
BRAKE_FIELD = 1.0
CFL_NUMBER = 0.1
LIFT = 30.0

STAGES = ((0.0, 1.0, 1.0), (0.75, 0.25, 0.25), (1.0 / 3.0, 2.0 / 3.0, 2.0 / 3.0))


def lgl_derivative():
    points = np.array(
        [
            -1.0,
            -0.7650553239294647,
            -0.2852315164806451,
            0.2852315164806451,
            0.7650553239294647,
            1.0,
        ]
    )
    count = points.shape[0]
    barycentric = np.ones(count)
    for row in range(count):
        for column in range(count):
            if row != column:
                barycentric[row] = barycentric[row] / (points[row] - points[column])
    matrix = np.zeros((count, count))
    for row in range(count):
        for column in range(count):
            if row != column:
                matrix[row, column] = (
                    barycentric[column] / barycentric[row] / (points[row] - points[column])
                )
    for row in range(count):
        matrix[row, row] = -np.sum(matrix[row])
    return matrix.astype(np.float32)


def volume_matrix():
    line = lgl_derivative().astype(np.float64)
    line[0, 0] += LIFT / 2
    line[5, 5] -= LIFT / 2
    line = -2.0 * line
    eye = np.eye(6)
    whole = np.zeros((PADDED, 3 * PADDED))
    whole[:NODES, :NODES] = np.kron(np.kron(line, eye), eye)
    whole[:NODES, PADDED : PADDED + NODES] = np.kron(np.kron(eye, line), eye)
    whole[:NODES, 2 * PADDED : 2 * PADDED + NODES] = np.kron(np.kron(eye, eye), line)
    whole = whole.astype(np.float32)
    high = whole.astype(jnp.bfloat16)
    low = (whole - high.astype(np.float32)).astype(jnp.bfloat16)
    return np.stack([high, low])


def root(x):
    return x * lax.rsqrt(jnp.maximum(x, 1e-30))


def primitives(u):
    inverse = 1.0 / u[0]
    velocity = [u[1] * inverse, u[2] * inverse, u[3] * inverse]
    kinetic = u[1] * velocity[0] + u[2] * velocity[1] + u[3] * velocity[2]
    squares = [u[5] * u[5], u[6] * u[6], u[7] * u[7]]
    field_sq = squares[0] + squares[1] + squares[2]
    pressure = (GAMMA - 1.0) * (u[4] - 0.5 * (kinetic + field_sq + u[8] * u[8]))
    return inverse, velocity, squares, field_sq, pressure


def fast_terms(prims):
    _, _, _, field_sq, pressure = prims
    acoustic = GAMMA * pressure
    gap = acoustic - field_sq
    return acoustic + field_sq, gap * gap, 4.0 * acoustic


def speed_along(prims, terms, d):
    inverse, velocity, squares, _, _ = prims
    both, gap_sq, acoustic4 = terms
    across = squares[(d + 1) % 3] + squares[(d + 2) % 3]
    inner = both + root(gap_sq + acoustic4 * across)
    return jnp.maximum(jnp.abs(velocity[d]) + root(0.5 * inverse * inner), GLM_SPEED)


def face_side(u, d):
    prims = primitives(u)
    _, velocity, _, field_sq, pressure = prims
    field = u[5:8]
    total = pressure + 0.5 * field_sq
    v, b = velocity[d], field[d]
    dot = velocity[0] * field[0] + velocity[1] * field[1] + velocity[2] * field[2]
    twice = GLM_SPEED * u[8]
    flux = [u[1 + d]]
    for c in range(3):
        entry = u[1 + c] * v - field[c] * b
        flux.append(entry + total if c == d else entry)
    flux.append(v * (u[4] + total) + b * (twice - dot))
    for c in range(3):
        flux.append(twice if c == d else v * field[c] - b * velocity[c])
    flux.append(GLM_SPEED * b)
    return flux, speed_along(prims, fast_terms(prims), d)


def face_flux(left, right, d):
    left_flux, left_speed = face_side(left, d)
    right_flux, right_speed = face_side(right, d)
    half = LIFT / 2
    largest = half * jnp.maximum(left_speed, right_speed)
    return [
        half * (left_flux[c] + right_flux[c]) - largest * (right[c] - left[c]) for c in range(9)
    ]


def inflow_value(c, d, outward):
    if c == 0:
        return 1.0
    if c == 1 + d:
        return -outward * JET_SPEED
    if c == 4:
        return 1.0 / (GAMMA - 1.0) + 0.5 * JET_SPEED**2 + 0.5 * BRAKE_FIELD**2
    if c == 7:
        return BRAKE_FIELD
    return 0.0


def with_outer(inner, interior, code, d, outward):
    states = []
    for c in range(9):
        x = interior[c]
        if c == 1 + d:
            x = jnp.where(code == 1, -x, x)
        x = jnp.where(code == 0, inflow_value(c, d, outward), x)
        states.append(x if inner is None else jnp.where(code < 3, x, inner[c]))
    return states


CHUNKS = ((0, 16), (16, 16), (32, 4))


def kernel(
    nlen,
    nwid,
    u_hbm,
    mat_hbm,
    ends_ref,
    sides_ref,
    walls_ref,
    out_ref,
    dt_ref,
    u0,
    u1,
    u2,
    mat,
    fhi,
    flo,
    acc,
    above,
    below,
    own_low,
    own_high,
    wide_below,
    wide_above,
    t_low,
    t_high,
    g_wide,
    e_low,
    e_high,
    peak,
    peak_group,
    peak_all,
    load_sem,
    send_sem,
    recv_sem,
    peak_send,
    peak_recv,
):
    li = lax.axis_index("len")
    wi = lax.axis_index("wid")
    group = max(nlen // 2, 1)
    blocks = nlen // group
    crowd = blocks * nwid
    lanes = lax.broadcasted_iota(jnp.int32, (1, LANES), 1)
    states = (u0, u1, u2)

    load_u = pltpu.make_async_copy(u_hbm, u0.at[:, pl.ds(0, NODES), :], load_sem.at[0])
    load_m = pltpu.make_async_copy(mat_hbm, mat, load_sem.at[1])
    load_u.start()
    load_m.start()

    in_group = lax.rem(li, group)
    block = li // group
    base = block * group
    in_crowd = block * nwid + wi

    def group_peer(step):
        return (base + lax.rem(in_group + step, group), wi)

    def crowd_peer(step):
        other = lax.rem(in_crowd + step, crowd)
        return ((other // nwid) * group + in_group, lax.rem(other, nwid))

    barrier = pltpu.get_barrier_semaphore()

    def greet(peer):
        pl.semaphore_signal(barrier, inc=1, device_id=peer, device_id_type=MESH)

    has_prev, has_next = li > 0, li < nlen - 1
    has_left, has_right = wi > 0, wi < nwid - 1

    @pl.when(has_prev)
    def _():
        greet((li - 1, wi))

    @pl.when(has_next)
    def _():
        greet((li + 1, wi))

    @pl.loop(1, group)
    def _(step):
        greet(group_peer(step))

    @pl.loop(1, crowd)
    def _(step):
        greet(crowd_peer(step))

    for ref in states:
        for c in range(9):
            ref[c, pl.ds(NODES, 8), :] = jnp.ones((8, LANES), jnp.float32)

    z = lanes % EZ
    y = lanes // EZ
    wide = LANES // EZ

    def tiled(row):
        return jnp.concatenate([row] * wide, axis=1)

    def wall_row(side):
        row = walls_ref[side]
        parts = [jnp.broadcast_to(row[:, q : q + 1], (1, EZ)) for q in range(wide)]
        return jnp.concatenate(parts, axis=1)

    def ends_row(side):
        return jnp.concatenate([ends_ref[side, q : q + 1, :] for q in range(wide)], axis=1)

    low_wall = jnp.where(z == 0, wall_row(0), 3)
    high_wall = wall_row(1)

    load_u.wait()
    neighbours = (
        has_prev.astype(jnp.int32)
        + has_next.astype(jnp.int32)
    )
    pl.semaphore_wait(barrier, group - 1 + crowd - 1 + neighbours)

    def copy_prev(s):
        return pltpu.make_async_remote_copy(
            src_ref=states[s].at[:, pl.ds(0, HALO), :],
            dst_ref=above.at[s],
            send_sem=send_sem.at[s, 0],
            recv_sem=recv_sem.at[s, 0],
            device_id=(li - 1, wi),
            device_id_type=MESH,
        )

    def copy_next(s):
        return pltpu.make_async_remote_copy(
            src_ref=states[s].at[:, pl.ds(NODES - HALO, HALO), :],
            dst_ref=below.at[s],
            send_sem=send_sem.at[s, 1],
            recv_sem=recv_sem.at[s, 1],
            device_id=(li + 1, wi),
            device_id_type=MESH,
        )

    def copy_left(s):
        return pltpu.make_async_remote_copy(
            src_ref=own_low.at[s],
            dst_ref=wide_above.at[s],
            send_sem=send_sem.at[s, 2],
            recv_sem=recv_sem.at[s, 2],
            device_id=(li, wi - 1),
            device_id_type=MESH,
        )

    def copy_right(s):
        return pltpu.make_async_remote_copy(
            src_ref=own_high.at[s],
            dst_ref=wide_below.at[s],
            send_sem=send_sem.at[s, 3],
            recv_sem=recv_sem.at[s, 3],
            device_id=(li, wi + 1),
            device_id_type=MESH,
        )

    def roll(x, by):
        by = by % LANES
        return x if by == 0 else pltpu.roll(x, by, axis=1)

    def packed(ref):
        return [ref[pl.ds(c, PACK, stride=9), :] for c in range(9)]

    def send(s):
        u = states[s]

        @pl.when(has_prev)
        def _():
            copy_prev(s).start()

        @pl.when(has_next)
        def _():
            copy_next(s).start()

        for c in range(9):
            for i in range(6):
                t_low[c, pl.ds(6 * i, 6), :] = u[c, pl.ds(36 * i, 6), :]
                t_high[c, pl.ds(6 * i, 6), :] = u[c, pl.ds(36 * i + 30, 6), :]
        for ref, dest, first in ((t_low, own_low, 0), (t_high, own_high, wide - 1)):
            for c in range(9):
                whole = None
                for q in range(wide):
                    piece = roll(ref[c, pl.ds(q, PACK, stride=4), :], EZ * (q - first))
                    whole = piece if q == 0 else jnp.where(y == q, piece, whole)
                dest[s, pl.ds(c, PACK, stride=9), :] = whole

        @pl.when(has_left)
        def _():
            copy_left(s).start()

        @pl.when(has_right)
        def _():
            copy_right(s).start()

    def volume(s):
        u_ref = states[s]

        def put(d, c, parts):
            fhi[pl.ds(rows[d], 16), pl.ds(c * LANES, LANES)] = parts[0]
            flo[pl.ds(rows[d], 16), pl.ds(c * LANES, LANES)] = parts[1]

        def split(x):
            high = x.astype(jnp.bfloat16)
            return high, (x - high.astype(jnp.float32)).astype(jnp.bfloat16)

        rows = [None] * 3

        def body(chunk, _):
            start = pl.multiple_of(chunk * 16, 16)
            for d in range(3):
                rows[d] = pl.multiple_of(d * PADDED + chunk * 16, 16)
            u = [u_ref[c, pl.ds(start, 16), :] for c in range(9)]
            prims = primitives(u)
            _, velocity, _, field_sq, pressure = prims
            field = u[5:8]
            total = pressure + 0.5 * field_sq
            enthalpy = u[4] + total
            twice = GLM_SPEED * u[8]
            back = twice - (
                velocity[0] * field[0] + velocity[1] * field[1] + velocity[2] * field[2]
            )
            psi_parts = split(twice)
            for d in range(3):
                put(d, 0, split(u[1 + d]))
                put(d, 5 + d, psi_parts)
                put(d, 8, split(GLM_SPEED * field[d]))
                put(d, 4, split(velocity[d] * enthalpy + field[d] * back))
                put(d, 1 + d, split(u[1 + d] * velocity[d] - field[d] * field[d] + total))
                for e in range(d + 1, 3):
                    shear = split(u[1 + d] * velocity[e] - field[d] * field[e])
                    put(d, 1 + e, shear)
                    put(e, 1 + d, shear)
                    turn = split(velocity[d] * field[e] - field[d] * velocity[e])
                    put(d, 5 + e, turn)
                    put(e, 5 + d, (-turn[0], -turn[1]))
            if s == 0:
                terms = fast_terms(prims)
                top = speed_along(prims, terms, 0)
                for d in (1, 2):
                    top = jnp.maximum(top, speed_along(prims, terms, d))
                row = lax.broadcasted_iota(jnp.int32, (16, LANES), 0) + start
                top = jnp.where(row < NODES, top, GLM_SPEED)
                peak[...] = jnp.maximum(peak[...], jnp.max(top, axis=0, keepdims=True))
            return 0

        lax.fori_loop(0, PADDED // 16, body, 0)

    def derivatives():
        for first in range(0, 9, 2):
            count = min(2, 9 - first)
            span = pl.ds(first * LANES, count * LANES)
            high = fhi[:, span]
            result = jnp.dot(mat[0], high, preferred_element_type=jnp.float32)
            result += jnp.dot(mat[1], high, preferred_element_type=jnp.float32)
            result += jnp.dot(mat[0], flo[:, span], preferred_element_type=jnp.float32)
            for c in range(count):
                acc[first + c] = result[:, c * LANES : (c + 1) * LANES]

    def inner_faces(s):
        u_ref = states[s]
        for first, count in CHUNKS:
            low_rows = pl.ds(6 * first, count, stride=6)
            high_rows = pl.ds(6 * first + 5, count, stride=6)
            low = [u_ref[c, low_rows, :] for c in range(9)]
            high = [u_ref[c, high_rows, :] for c in range(9)]
            beside = [roll(x, 1) for x in high]
            left = with_outer(beside, low, low_wall, 2, -1.0)
            flux = face_flux(left, low, 2)
            for c in range(9):
                acc[c, low_rows, :] = acc[c, low_rows, :] + flux[c]
            last = face_flux(high, with_outer(None, high, high_wall, 2, 1.0), 2)
            for c in range(9):
                upper = jnp.where(z == EZ - 1, last[c], roll(flux[c], -1))
                acc[c, high_rows, :] = acc[c, high_rows, :] - upper
        for first, count in CHUNKS:
            rows = pl.ds(first, count)
            low = [t_low[c, rows, :] for c in range(9)]
            left = [roll(t_high[c, rows, :], EZ) for c in range(9)]
            flux = face_flux(left, low, 1)
            for c in range(9):
                g_wide[c, rows, :] = flux[c]
        for c in range(9):
            for i in range(6):
                flux = g_wide[c, pl.ds(6 * i, 6), :]
                rows = pl.ds(36 * i, 6)
                acc[c, rows, :] = acc[c, rows, :] + jnp.where(y > 0, flux, 0.0)
                rows = pl.ds(36 * i + 30, 6)
                acc[c, rows, :] = acc[c, rows, :] - jnp.where(y < wide - 1, roll(flux, -EZ), 0.0)

    def width_edges(s):
        @pl.when(has_left)
        def _():
            copy_right(s).wait_recv()

        @pl.when(has_right)
        def _():
            copy_left(s).wait_recv()

        @pl.when(jnp.logical_not(has_left))
        def _():
            outer = with_outer(None, packed(own_low.at[s]), tiled(sides_ref[0]), 1, -1.0)
            for c in range(9):
                wide_below[s, pl.ds(c, PACK, stride=9), :] = outer[c]

        @pl.when(jnp.logical_not(has_right))
        def _():
            outer = with_outer(None, packed(own_high.at[s]), tiled(sides_ref[1]), 1, 1.0)
            for c in range(9):
                wide_above[s, pl.ds(c, PACK, stride=9), :] = outer[c]

        low = face_flux(packed(wide_below.at[s]), packed(own_low.at[s]), 1)
        high = face_flux(packed(own_high.at[s]), packed(wide_above.at[s]), 1)
        for c in range(9):
            for q in range(wide):
                rows = pl.ds(q, PACK, stride=4)
                e_low[c, rows, :] = jnp.where(y == 0, roll(low[c], -EZ * q), 0.0)
                e_high[c, rows, :] = jnp.where(
                    y == wide - 1, roll(high[c], EZ * (wide - 1 - q)), 0.0
                )
        for c in range(9):
            for i in range(6):
                rows = pl.ds(36 * i, 6)
                acc[c, rows, :] = acc[c, rows, :] + e_low[c, pl.ds(6 * i, 6), :]
                rows = pl.ds(36 * i + 30, 6)
                acc[c, rows, :] = acc[c, rows, :] - e_high[c, pl.ds(6 * i, 6), :]

    def length_edges(s):
        u_ref = states[s]
        top = NODES - FACE
        skip = HALO - FACE

        @pl.when(has_prev)
        def _():
            copy_next(s).wait_recv()

        @pl.when(has_next)
        def _():
            copy_prev(s).wait_recv()

        @pl.when(jnp.logical_not(has_prev))
        def _():
            for first, count in CHUNKS:
                own = [u_ref[c, pl.ds(first, count), :] for c in range(9)]
                outer = with_outer(None, own, ends_row(0), 0, -1.0)
                for c in range(9):
                    below[s, c, pl.ds(skip + first, count), :] = outer[c]

        @pl.when(jnp.logical_not(has_next))
        def _():
            for first, count in CHUNKS:
                own = [u_ref[c, pl.ds(top + first, count), :] for c in range(9)]
                outer = with_outer(None, own, ends_row(1), 0, 1.0)
                for c in range(9):
                    above[s, c, pl.ds(first, count), :] = outer[c]

        for first, count in CHUNKS:
            rows = pl.ds(first, count)
            left = [below[s, c, pl.ds(skip + first, count), :] for c in range(9)]
            flux = face_flux(left, [u_ref[c, rows, :] for c in range(9)], 0)
            for c in range(9):
                acc[c, rows, :] = acc[c, rows, :] + flux[c]
        for first, count in CHUNKS:
            rows = pl.ds(top + first, count)
            right = [above[s, c, pl.ds(first, count), :] for c in range(9)]
            flux = face_flux([u_ref[c, rows, :] for c in range(9)], right, 0)
            for c in range(9):
                acc[c, rows, :] = acc[c, rows, :] - flux[c]

    def update(s, step):
        first, own, factor = STAGES[s]
        weight = step * factor
        for c in range(9):
            rows = pl.ds(0, NODES)
            new = own * states[s][c, rows, :] + weight * acc[c, rows, :]
            if first:
                new = new + first * u0[c, rows, :]
            if s < 2:
                states[s + 1][c, rows, :] = new
            else:
                out_ref[c] = new

    def peak_copy(src, dst, which, step, peer):
        return pltpu.make_async_remote_copy(
            src_ref=src,
            dst_ref=dst.at[step - 1],
            send_sem=peak_send.at[which],
            recv_sem=peak_recv.at[which],
            device_id=peer,
            device_id_type=MESH,
        )

    peak[...] = jnp.full((1, LANES), GLM_SPEED, jnp.float32)
    send(0)
    volume(0)

    @pl.loop(1, group)
    def _(step):
        peak_copy(peak, peak_group, 0, step, group_peer(step)).start()

    load_m.wait()
    derivatives()
    pltpu.make_async_copy(peak_group, peak_group, peak_recv.at[0]).wait()
    pltpu.make_async_copy(peak_group, peak_group, peak_send.at[0]).wait()
    peak[...] = jnp.maximum(peak[...], jnp.max(peak_group[...], axis=0))

    @pl.loop(1, crowd)
    def _(step):
        peak_copy(peak, peak_all, 1, step, crowd_peer(step)).start()

    inner_faces(0)
    width_edges(0)
    length_edges(0)
    pltpu.make_async_copy(peak_all, peak_all, peak_recv.at[1]).wait()
    fastest = jnp.max(jnp.maximum(peak[...], jnp.max(peak_all[...], axis=0)), axis=1, keepdims=True)
    step_row = CFL_NUMBER / (11.0 * jnp.broadcast_to(fastest, (1, LANES)))
    dt_ref[0, 0] = jnp.max(step_row)
    update(0, step_row)

    for s in (1, 2):
        send(s)
        volume(s)
        derivatives()
        inner_faces(s)
        width_edges(s)
        length_edges(s)
        update(s, step_row)

    pltpu.make_async_copy(peak_all, peak_all, peak_send.at[1]).wait()
    for s in range(3):
        for have, copy in (
            (has_prev, copy_prev),
            (has_next, copy_next),
            (has_left, copy_left),
            (has_right, copy_right),
        ):

            @pl.when(have)
            def _(copy=copy):
                copy(s).wait_send()


def solution(mesh):
    nlen, nwid = mesh.shape["len"], mesh.shape["wid"]
    group = max(nlen // 2, 1)
    crowd = nlen // group * nwid
    matrix = volume_matrix()

    def on_device(conserved, ends_kind, sides_kind, walls_kind):
        f32 = jnp.float32
        vmem = pl.BlockSpec(memory_space=pltpu.VMEM)
        hbm = pl.BlockSpec(memory_space=pl.ANY)
        state = pltpu.VMEM((9, PADDED, LANES), f32)
        halo = pltpu.VMEM((3, 9, HALO, LANES), f32)
        pack = pltpu.VMEM((3, 9 * PACK, LANES), f32)
        trace = pltpu.VMEM((9, HALO, LANES), f32)
        flux = pltpu.VMEM((3 * PADDED, 9 * LANES), jnp.bfloat16)
        updated, step = pl.pallas_call(
            functools.partial(kernel, nlen, nwid),
            out_shape=(
                jax.ShapeDtypeStruct((9, NODES, LANES), f32),
                jax.ShapeDtypeStruct((1, 1), f32),
            ),
            in_specs=[hbm, hbm, vmem, vmem, vmem],
            out_specs=(vmem, pl.BlockSpec(memory_space=pltpu.SMEM)),
            scratch_shapes=[
                state,
                state,
                state,
                pltpu.VMEM((2, PADDED, 3 * PADDED), jnp.bfloat16),
                flux,
                flux,
                state,
                halo,
                halo,
                pack,
                pack,
                pack,
                pack,
                trace,
                trace,
                trace,
                trace,
                trace,
                pltpu.VMEM((1, LANES), f32),
                pltpu.VMEM((group - 1, 1, LANES), f32),
                pltpu.VMEM((crowd - 1, 1, LANES), f32),
                pltpu.SemaphoreType.DMA((2,)),
                pltpu.SemaphoreType.DMA((3, 4)),
                pltpu.SemaphoreType.DMA((3, 4)),
                pltpu.SemaphoreType.DMA((2,)),
                pltpu.SemaphoreType.DMA((2,)),
            ],
            compiler_params=pltpu.CompilerParams(
                collective_id=0, has_side_effects=True, vmem_limit_bytes=40 * 1024 * 1024
            ),
        )(
            conserved.reshape(9, NODES, LANES),
            jnp.asarray(matrix),
            ends_kind,
            sides_kind,
            walls_kind,
        )
        return updated.reshape(conserved.shape), step.reshape(())

    return jax.shard_map(
        on_device,
        mesh=mesh,
        in_specs=(
            P(None, None, None, None, "len", "wid"),
            P(None, "wid", None),
            P(None, "len", None),
            P(None, "len", "wid"),
        ),
        out_specs=(P(None, None, None, None, "len", "wid"), P()),
        check_vma=False,
    )
```

```python
import functools

import jax
import jax.numpy as jnp
import numpy as np
from jax import lax
from jax.experimental import pallas as pl
from jax.experimental.pallas import tpu as pltpu
from jax.sharding import PartitionSpec as P

MESH = pl.DeviceIdType.MESH

EZ = 32
LANES = 128
NODES = 216
PADDED = 224
FACE = 36
HALO = 40
PACK = 9

GAMMA = 5.0 / 3.0
GLM_SPEED = 2.0
JET_SPEED = 0.8
BRAKE_FIELD = 1.0
CFL_NUMBER = 0.1
LIFT = 30.0

STAGES = ((0.0, 1.0, 1.0), (0.75, 0.25, 0.25), (1.0 / 3.0, 2.0 / 3.0, 2.0 / 3.0))


def lgl_derivative():
    points = np.array(
        [
            -1.0,
            -0.7650553239294647,
            -0.2852315164806451,
            0.2852315164806451,
            0.7650553239294647,
            1.0,
        ]
    )
    count = points.shape[0]
    barycentric = np.ones(count)
    for row in range(count):
        for column in range(count):
            if row != column:
                barycentric[row] = barycentric[row] / (points[row] - points[column])
    matrix = np.zeros((count, count))
    for row in range(count):
        for column in range(count):
            if row != column:
                matrix[row, column] = (
                    barycentric[column] / barycentric[row] / (points[row] - points[column])
                )
    for row in range(count):
        matrix[row, row] = -np.sum(matrix[row])
    return matrix.astype(np.float32)


def volume_matrix():
    line = lgl_derivative().astype(np.float64)
    line[0, 0] += LIFT / 2
    line[5, 5] -= LIFT / 2
    line = -2.0 * line
    eye = np.eye(6)
    whole = np.zeros((PADDED, 3 * PADDED))
    whole[:NODES, :NODES] = np.kron(np.kron(line, eye), eye)
    whole[:NODES, PADDED : PADDED + NODES] = np.kron(np.kron(eye, line), eye)
    whole[:NODES, 2 * PADDED : 2 * PADDED + NODES] = np.kron(np.kron(eye, eye), line)
    whole = whole.astype(np.float32)
    high = whole.astype(jnp.bfloat16)
    low = (whole - high.astype(np.float32)).astype(jnp.bfloat16)
    return np.stack([high, low])


def root(x):
    return x * lax.rsqrt(jnp.maximum(x, 1e-30))


def primitives(u):
    inverse = 1.0 / u[0]
    velocity = [u[1] * inverse, u[2] * inverse, u[3] * inverse]
    kinetic = u[1] * velocity[0] + u[2] * velocity[1] + u[3] * velocity[2]
    squares = [u[5] * u[5], u[6] * u[6], u[7] * u[7]]
    field_sq = squares[0] + squares[1] + squares[2]
    pressure = (GAMMA - 1.0) * (u[4] - 0.5 * (kinetic + field_sq + u[8] * u[8]))
    return inverse, velocity, squares, field_sq, pressure


def fast_terms(prims):
    _, _, _, field_sq, pressure = prims
    acoustic = GAMMA * pressure
    gap = acoustic - field_sq
    return acoustic + field_sq, gap * gap, 4.0 * acoustic


def speed_along(prims, terms, d):
    inverse, velocity, squares, _, _ = prims
    both, gap_sq, acoustic4 = terms
    across = squares[(d + 1) % 3] + squares[(d + 2) % 3]
    inner = both + root(gap_sq + acoustic4 * across)
    return jnp.maximum(jnp.abs(velocity[d]) + root(0.5 * inverse * inner), GLM_SPEED)


def face_side(u, d):
    prims = primitives(u)
    _, velocity, _, field_sq, pressure = prims
    field = u[5:8]
    total = pressure + 0.5 * field_sq
    v, b = velocity[d], field[d]
    dot = velocity[0] * field[0] + velocity[1] * field[1] + velocity[2] * field[2]
    twice = GLM_SPEED * u[8]
    flux = [u[1 + d]]
    for c in range(3):
        entry = u[1 + c] * v - field[c] * b
        flux.append(entry + total if c == d else entry)
    flux.append(v * (u[4] + total) + b * (twice - dot))
    for c in range(3):
        flux.append(twice if c == d else v * field[c] - b * velocity[c])
    flux.append(GLM_SPEED * b)
    return flux, speed_along(prims, fast_terms(prims), d)


def face_flux(left, right, d):
    left_flux, left_speed = face_side(left, d)
    right_flux, right_speed = face_side(right, d)
    half = LIFT / 2
    largest = half * jnp.maximum(left_speed, right_speed)
    return [
        half * (left_flux[c] + right_flux[c]) - largest * (right[c] - left[c]) for c in range(9)
    ]


def inflow_value(c, d, outward):
    if c == 0:
        return 1.0
    if c == 1 + d:
        return -outward * JET_SPEED
    if c == 4:
        return 1.0 / (GAMMA - 1.0) + 0.5 * JET_SPEED**2 + 0.5 * BRAKE_FIELD**2
    if c == 7:
        return BRAKE_FIELD
    return 0.0


def with_outer(inner, interior, code, d, outward):
    states = []
    for c in range(9):
        x = interior[c]
        if c == 1 + d:
            x = jnp.where(code == 1, -x, x)
        x = jnp.where(code == 0, inflow_value(c, d, outward), x)
        states.append(x if inner is None else jnp.where(code < 3, x, inner[c]))
    return states


CHUNKS = ((0, 16), (16, 16), (32, 4))


def kernel(
    nlen,
    nwid,
    u_hbm,
    mat_hbm,
    ends_hbm,
    sides_hbm,
    walls_hbm,
    out_ref,
    dt_ref,
    ends_ref,
    sides_ref,
    walls_ref,
    u0,
    u1,
    u2,
    mat,
    fhi,
    flo,
    acc,
    above,
    below,
    own_low,
    own_high,
    wide_below,
    wide_above,
    t_low,
    t_high,
    g_wide,
    peak,
    peak_group,
    peak_all,
    load_sem,
    send_sem,
    recv_sem,
    peak_send,
    peak_recv,
):
    li = lax.axis_index("len")
    wi = lax.axis_index("wid")
    group = max(nlen // 2, 1)
    blocks = nlen // group
    crowd = blocks * nwid
    lanes = lax.broadcasted_iota(jnp.int32, (1, LANES), 1)
    states = (u0, u1, u2, out_ref)

    load_u = pltpu.make_async_copy(u_hbm, u0.at[:, pl.ds(0, NODES), :], load_sem.at[0])
    load_m = pltpu.make_async_copy(mat_hbm, mat, load_sem.at[1])
    load_u.start()
    load_kinds = [
        pltpu.make_async_copy(src, dst, load_sem.at[2 + n])
        for n, (src, dst) in enumerate(
            ((ends_hbm, ends_ref), (sides_hbm, sides_ref), (walls_hbm, walls_ref))
        )
    ]
    for load in load_kinds:
        load.start()
    load_m.start()

    in_group = lax.rem(li, group)
    block = li // group
    base = block * group
    in_crowd = block * nwid + wi

    def group_peer(step):
        return (base + lax.rem(in_group + step, group), wi)

    def crowd_peer(step):
        other = lax.rem(in_crowd + step, crowd)
        return ((other // nwid) * group + in_group, lax.rem(other, nwid))

    barrier = pltpu.get_barrier_semaphore()

    def greet(peer):
        pl.semaphore_signal(barrier, inc=1, device_id=peer, device_id_type=MESH)

    has_prev, has_next = li > 0, li < nlen - 1
    has_left, has_right = wi > 0, wi < nwid - 1

    for step in range(1, crowd // 2 + 1):
        greet(crowd_peer(step))
        if step < crowd - step:
            greet(crowd_peer(crowd - step))

    @pl.when(has_prev)
    def _():
        greet((li - 1, wi))

    @pl.when(has_next)
    def _():
        greet((li + 1, wi))

    @pl.loop(1, group)
    def _(step):
        greet(group_peer(step))

    for ref in states[:3]:
        for c in range(9):
            ref[c, pl.ds(NODES, 8), :] = jnp.ones((8, LANES), jnp.float32)

    z = lanes % EZ
    y = lanes // EZ
    wide = LANES // EZ

    def tiled(row):
        return jnp.concatenate([row] * wide, axis=1)

    def wall_row(side):
        row = walls_ref[side]
        parts = [jnp.broadcast_to(row[:, q : q + 1], (1, EZ)) for q in range(wide)]
        return jnp.concatenate(parts, axis=1)

    def ends_row(side):
        return jnp.concatenate([ends_ref[side, q : q + 1, :] for q in range(wide)], axis=1)


    def copy_prev(s):
        return pltpu.make_async_remote_copy(
            src_ref=states[s].at[:, pl.ds(0, HALO), :],
            dst_ref=above.at[s],
            send_sem=send_sem.at[s, 0],
            recv_sem=recv_sem.at[s, 0],
            device_id=(li - 1, wi),
            device_id_type=MESH,
        )

    def copy_next(s):
        return pltpu.make_async_remote_copy(
            src_ref=states[s].at[:, pl.ds(NODES - HALO, HALO), :],
            dst_ref=below.at[s],
            send_sem=send_sem.at[s, 1],
            recv_sem=recv_sem.at[s, 1],
            device_id=(li + 1, wi),
            device_id_type=MESH,
        )

    def copy_left(s):
        return pltpu.make_async_remote_copy(
            src_ref=own_low.at[s],
            dst_ref=wide_above.at[s],
            send_sem=send_sem.at[s, 2],
            recv_sem=recv_sem.at[s, 2],
            device_id=(li, wi - 1),
            device_id_type=MESH,
        )

    def copy_right(s):
        return pltpu.make_async_remote_copy(
            src_ref=own_high.at[s],
            dst_ref=wide_below.at[s],
            send_sem=send_sem.at[s, 3],
            recv_sem=recv_sem.at[s, 3],
            device_id=(li, wi + 1),
            device_id_type=MESH,
        )

    def roll(x, by):
        by = by % LANES
        return x if by == 0 else pltpu.roll(x, by, axis=1)

    def packed(ref):
        return [ref[pl.ds(c, PACK, stride=9), :] for c in range(9)]

    def send_width(s):
        @pl.when(has_left)
        def _():
            copy_left(s).start()

        @pl.when(has_right)
        def _():
            copy_right(s).start()

    def send_length(s):
        @pl.when(has_prev)
        def _():
            copy_prev(s).start()

        @pl.when(has_next)
        def _():
            copy_next(s).start()

    def gather(s):
        u = states[s]
        for c in range(9):
            for i in range(6):
                t_low[c, pl.ds(6 * i, 6), :] = u[c, pl.ds(36 * i, 6), :]
                t_high[c, pl.ds(6 * i, 6), :] = u[c, pl.ds(36 * i + 30, 6), :]
        for ref, dest, first in ((t_low, own_low, 0), (t_high, own_high, wide - 1)):
            for c in range(9):
                whole = None
                for q in range(wide):
                    piece = roll(ref[c, pl.ds(q, PACK, stride=4), :], EZ * (q - first))
                    whole = piece if q == 0 else jnp.where(y == q, piece, whole)
                dest[s, pl.ds(c, PACK, stride=9), :] = whole

    def scatter(s):
        u = states[s]
        for ref, src, first in ((t_low, own_low, 0), (t_high, own_high, wide - 1)):
            for c in range(9):
                new = src[s, pl.ds(c, PACK, stride=9), :]
                for q in range(wide):
                    rows = pl.ds(q, PACK, stride=4)
                    ref[c, rows, :] = jnp.where(
                        y == first, roll(new, EZ * (first - q)), ref[c, rows, :]
                    )
        for c in range(9):
            for i in range(6):
                u[c, pl.ds(36 * i, 6), :] = t_low[c, pl.ds(6 * i, 6), :]
                u[c, pl.ds(36 * i + 30, 6), :] = t_high[c, pl.ds(6 * i, 6), :]

    def volume(s):
        u_ref = states[s]

        def put(d, c, parts):
            fhi[pl.ds(rows[d], 16), pl.ds(c * LANES, LANES)] = parts[0]
            flo[pl.ds(rows[d], 16), pl.ds(c * LANES, LANES)] = parts[1]

        def split(x):
            high = x.astype(jnp.bfloat16)
            return high, (x - high.astype(jnp.float32)).astype(jnp.bfloat16)

        rows = [None] * 3

        def body(chunk, _):
            start = pl.multiple_of(chunk * 16, 16)
            for d in range(3):
                rows[d] = pl.multiple_of(d * PADDED + chunk * 16, 16)
            u = [u_ref[c, pl.ds(start, 16), :] for c in range(9)]
            prims = primitives(u)
            _, velocity, _, field_sq, pressure = prims
            field = u[5:8]
            total = pressure + 0.5 * field_sq
            enthalpy = u[4] + total
            twice = GLM_SPEED * u[8]
            back = twice - (
                velocity[0] * field[0] + velocity[1] * field[1] + velocity[2] * field[2]
            )
            psi_parts = split(twice)
            for d in range(3):
                put(d, 0, split(u[1 + d]))
                put(d, 5 + d, psi_parts)
                put(d, 8, split(GLM_SPEED * field[d]))
                put(d, 4, split(velocity[d] * enthalpy + field[d] * back))
                put(d, 1 + d, split(u[1 + d] * velocity[d] - field[d] * field[d] + total))
                for e in range(d + 1, 3):
                    shear = split(u[1 + d] * velocity[e] - field[d] * field[e])
                    put(d, 1 + e, shear)
                    put(e, 1 + d, shear)
                    turn = split(velocity[d] * field[e] - field[d] * velocity[e])
                    put(d, 5 + e, turn)
                    put(e, 5 + d, (-turn[0], -turn[1]))
            return 0

        lax.fori_loop(0, PADDED // 16, body, 0)

    def largest_speed():
        def body(chunk, top):
            start = pl.multiple_of(chunk * 8, 8)
            prims = primitives([u0[c, pl.ds(start, 8), :] for c in range(9)])
            terms = fast_terms(prims)
            for d in range(3):
                top = jnp.maximum(top, speed_along(prims, terms, d))
            return top

        start = jnp.full((8, LANES), GLM_SPEED, jnp.float32)
        top = lax.fori_loop(0, NODES // 8, body, start, unroll=3)
        peak[...] = jnp.max(top, axis=0, keepdims=True)

    def derivatives():
        for first in range(0, 9, 2):
            count = min(2, 9 - first)
            span = pl.ds(first * LANES, count * LANES)
            high = fhi[:, span]
            result = jnp.dot(mat[0], high, preferred_element_type=jnp.float32)
            result += jnp.dot(mat[1], high, preferred_element_type=jnp.float32)
            result += jnp.dot(mat[0], flo[:, span], preferred_element_type=jnp.float32)
            for c in range(count):
                acc[first + c] = result[:, c * LANES : (c + 1) * LANES]

    def inner_faces(s, low_wall, high_wall):
        u_ref = states[s]
        for first, count in CHUNKS:
            low_rows = pl.ds(6 * first, count, stride=6)
            high_rows = pl.ds(6 * first + 5, count, stride=6)
            low = [u_ref[c, low_rows, :] for c in range(9)]
            high = [u_ref[c, high_rows, :] for c in range(9)]
            beside = [roll(x, 1) for x in high]
            left = with_outer(beside, low, low_wall, 2, -1.0)
            flux = face_flux(left, low, 2)
            for c in range(9):
                acc[c, low_rows, :] = acc[c, low_rows, :] + flux[c]
            last = face_flux(high, with_outer(None, high, high_wall, 2, 1.0), 2)
            for c in range(9):
                upper = jnp.where(z == EZ - 1, last[c], roll(flux[c], -1))
                acc[c, high_rows, :] = acc[c, high_rows, :] - upper
        for first, count in CHUNKS:
            rows = pl.ds(first, count)
            low = [t_low[c, rows, :] for c in range(9)]
            left = [roll(t_high[c, rows, :], EZ) for c in range(9)]
            flux = face_flux(left, low, 1)
            for c in range(9):
                g_wide[c, rows, :] = flux[c]
        for c in range(9):
            for i in range(6):
                flux = g_wide[c, pl.ds(6 * i, 6), :]
                rows = pl.ds(36 * i, 6)
                acc[c, rows, :] = acc[c, rows, :] + jnp.where(y > 0, flux, 0.0)
                rows = pl.ds(36 * i + 30, 6)
                acc[c, rows, :] = acc[c, rows, :] - jnp.where(y < wide - 1, roll(flux, -EZ), 0.0)

    def width_edges(s, step_row):
        @pl.when(has_left)
        def _():
            copy_right(s).wait_recv()

        @pl.when(has_right)
        def _():
            copy_left(s).wait_recv()

        @pl.when(jnp.logical_not(has_left))
        def _():
            outer = with_outer(None, packed(own_low.at[s]), tiled(sides_ref[0]), 1, -1.0)
            for c in range(9):
                wide_below[s, pl.ds(c, PACK, stride=9), :] = outer[c]

        @pl.when(jnp.logical_not(has_right))
        def _():
            outer = with_outer(None, packed(own_high.at[s]), tiled(sides_ref[1]), 1, 1.0)
            for c in range(9):
                wide_above[s, pl.ds(c, PACK, stride=9), :] = outer[c]

        weight = step_row * STAGES[s][2]
        for c, flux in enumerate(
            face_flux(packed(wide_below.at[s]), packed(own_low.at[s]), 1)
        ):
            rows = pl.ds(c, PACK, stride=9)
            own_low[s + 1, rows, :] = own_low[s + 1, rows, :] + weight * flux
        for c, flux in enumerate(
            face_flux(packed(own_high.at[s]), packed(wide_above.at[s]), 1)
        ):
            rows = pl.ds(c, PACK, stride=9)
            own_high[s + 1, rows, :] = own_high[s + 1, rows, :] - weight * flux

    def length_edges(s):
        u_ref = states[s]
        top = NODES - FACE
        skip = HALO - FACE

        @pl.when(has_prev)
        def _():
            copy_next(s).wait_recv()

        @pl.when(has_next)
        def _():
            copy_prev(s).wait_recv()

        @pl.when(jnp.logical_not(has_prev))
        def _():
            for first, count in CHUNKS:
                own = [u_ref[c, pl.ds(first, count), :] for c in range(9)]
                outer = with_outer(None, own, ends_row(0), 0, -1.0)
                for c in range(9):
                    below[s, c, pl.ds(skip + first, count), :] = outer[c]

        @pl.when(jnp.logical_not(has_next))
        def _():
            for first, count in CHUNKS:
                own = [u_ref[c, pl.ds(top + first, count), :] for c in range(9)]
                outer = with_outer(None, own, ends_row(1), 0, 1.0)
                for c in range(9):
                    above[s, c, pl.ds(first, count), :] = outer[c]

        for first, count in CHUNKS:
            rows = pl.ds(first, count)
            left = [below[s, c, pl.ds(skip + first, count), :] for c in range(9)]
            flux = face_flux(left, [u_ref[c, rows, :] for c in range(9)], 0)
            for c in range(9):
                acc[c, rows, :] = acc[c, rows, :] + flux[c]
        for first, count in CHUNKS:
            rows = pl.ds(top + first, count)
            right = [above[s, c, pl.ds(first, count), :] for c in range(9)]
            flux = face_flux([u_ref[c, rows, :] for c in range(9)], right, 0)
            for c in range(9):
                acc[c, rows, :] = acc[c, rows, :] - flux[c]

    def update(s, step, spans):
        first, own, factor = STAGES[s]
        weight = step * factor
        for start, count in spans:
            for c in range(9):
                rows = pl.ds(start, count)
                new = own * states[s][c, rows, :] + weight * acc[c, rows, :]
                if first:
                    new = new + first * u0[c, rows, :]
                states[s + 1][c, rows, :] = new

    def peak_copy(src, dst, which, step, peer):
        return pltpu.make_async_remote_copy(
            src_ref=src,
            dst_ref=dst.at[step - 1],
            send_sem=peak_send.at[which],
            recv_sem=peak_recv.at[which],
            device_id=peer,
            device_id_type=MESH,
        )

    inner_rows = ((HALO, NODES - 2 * HALO),)
    outer_rows = ((0, HALO), (NODES - HALO, HALO))

    load_u.wait()
    largest_speed()
    gather(0)
    for load in load_kinds:
        load.wait()
    low_wall = jnp.where(z == 0, wall_row(0), 3)
    high_wall = wall_row(1)
    neighbours = has_prev.astype(jnp.int32) + has_next.astype(jnp.int32)
    pl.semaphore_wait(barrier, group - 1 + crowd - 1 + neighbours)
    send_width(0)

    @pl.loop(1, group)
    def _(step):
        peak_copy(peak, peak_group, 0, step, group_peer(step)).start()

    step_row = None
    for s in range(3):
        send_length(s)
        volume(s)
        if s == 0:
            load_m.wait()
        derivatives()
        if s == 0:
            pltpu.make_async_copy(peak_group, peak_group, peak_recv.at[0]).wait()
            pltpu.make_async_copy(peak_group, peak_group, peak_send.at[0]).wait()
            peak[...] = jnp.maximum(peak[...], jnp.max(peak_group[...], axis=0))

            @pl.loop(1, crowd)
            def _(step):
                peak_copy(peak, peak_all, 1, step, crowd_peer(step)).start()

        inner_faces(s, low_wall, high_wall)
        if s:
            update(s, step_row, inner_rows)
        length_edges(s)
        if s == 0:
            pltpu.make_async_copy(peak_all, peak_all, peak_recv.at[1]).wait()
            fastest = jnp.maximum(peak[...], jnp.max(peak_all[...], axis=0))
            fastest = jnp.max(fastest, axis=1, keepdims=True)
            step_row = CFL_NUMBER / (11.0 * jnp.broadcast_to(fastest, (1, LANES)))
            dt_ref[0, 0] = jnp.max(step_row)
            update(s, step_row, inner_rows)
        update(s, step_row, outer_rows)
        gather(s + 1)
        width_edges(s, step_row)
        if s < 2:
            send_width(s + 1)
        scatter(s + 1)

    pltpu.make_async_copy(peak_all, peak_all, peak_send.at[1]).wait()
    for s in range(3):
        for have, copy in (
            (has_prev, copy_prev),
            (has_next, copy_next),
            (has_left, copy_left),
            (has_right, copy_right),
        ):

            @pl.when(have)
            def _(copy=copy):
                copy(s).wait_send()


def solution(mesh):
    nlen, nwid = mesh.shape["len"], mesh.shape["wid"]
    group = max(nlen // 2, 1)
    crowd = nlen // group * nwid
    matrix = volume_matrix()

    def on_device(conserved, ends_kind, sides_kind, walls_kind):
        f32 = jnp.float32
        vmem = pl.BlockSpec(memory_space=pltpu.VMEM)
        hbm = pl.BlockSpec(memory_space=pl.ANY)
        state = pltpu.VMEM((9, PADDED, LANES), f32)
        halo = pltpu.VMEM((3, 9, HALO, LANES), f32)
        pack = pltpu.VMEM((3, 9 * PACK, LANES), f32)
        own_pack = pltpu.VMEM((4, 9 * PACK, LANES), f32)
        trace = pltpu.VMEM((9, HALO, LANES), f32)
        flux = pltpu.VMEM((3 * PADDED, 9 * LANES), jnp.bfloat16)
        updated, step = pl.pallas_call(
            functools.partial(kernel, nlen, nwid),
            out_shape=(
                jax.ShapeDtypeStruct((9, NODES, LANES), f32),
                jax.ShapeDtypeStruct((1, 1), f32),
            ),
            in_specs=[hbm] * 5,
            out_specs=(vmem, pl.BlockSpec(memory_space=pltpu.SMEM)),
            scratch_shapes=[
                pltpu.VMEM((2, LANES // EZ, EZ), jnp.int32),
                pltpu.VMEM((2, 1, EZ), jnp.int32),
                pltpu.VMEM((2, 1, LANES // EZ), jnp.int32),
                state,
                state,
                state,
                pltpu.VMEM((2, PADDED, 3 * PADDED), jnp.bfloat16),
                flux,
                flux,
                state,
                halo,
                halo,
                own_pack,
                own_pack,
                pack,
                pack,
                trace,
                trace,
                trace,
                pltpu.VMEM((1, LANES), f32),
                pltpu.VMEM((max(group - 1, 1), 1, LANES), f32),
                pltpu.VMEM((max(crowd - 1, 1), 1, LANES), f32),
                pltpu.SemaphoreType.DMA((5,)),
                pltpu.SemaphoreType.DMA((3, 4)),
                pltpu.SemaphoreType.DMA((3, 4)),
                pltpu.SemaphoreType.DMA((2,)),
                pltpu.SemaphoreType.DMA((2,)),
            ],
            compiler_params=pltpu.CompilerParams(
                collective_id=0, has_side_effects=True, vmem_limit_bytes=40 * 1024 * 1024
            ),
        )(
            *(
                pltpu.with_memory_space_constraint(x, pltpu.HBM)
                for x in (
                    conserved.reshape(9, NODES, LANES),
                    jnp.asarray(matrix),
                    ends_kind,
                    sides_kind,
                    walls_kind,
                )
            )
        )
        return updated.reshape(conserved.shape), step.reshape(())

    return jax.shard_map(
        on_device,
        mesh=mesh,
        in_specs=(
            P(None, None, None, None, "len", "wid"),
            P(None, "wid", None),
            P(None, "len", None),
            P(None, "len", "wid"),
        ),
        out_specs=(P(None, None, None, None, "len", "wid"), P()),
        check_vma=False,
    )
```

```python
import functools

import jax
import jax.numpy as jnp
import numpy as np
from jax import lax
from jax.experimental import pallas as pl
from jax.experimental.pallas import tpu as pltpu
from jax.sharding import PartitionSpec as P

MESH = pl.DeviceIdType.MESH

EZ = 32
LANES = 128
NODES = 216
PADDED = 224
FACE = 36
HALO = 40
PACK = 9

GAMMA = 5.0 / 3.0
GLM_SPEED = 2.0
JET_SPEED = 0.8
BRAKE_FIELD = 1.0
CFL_NUMBER = 0.1
LIFT = 30.0

STAGES = ((0.0, 1.0, 1.0), (0.75, 0.25, 0.25), (1.0 / 3.0, 2.0 / 3.0, 2.0 / 3.0))


def lgl_derivative():
    points = np.array(
        [
            -1.0,
            -0.7650553239294647,
            -0.2852315164806451,
            0.2852315164806451,
            0.7650553239294647,
            1.0,
        ]
    )
    count = points.shape[0]
    barycentric = np.ones(count)
    for row in range(count):
        for column in range(count):
            if row != column:
                barycentric[row] = barycentric[row] / (points[row] - points[column])
    matrix = np.zeros((count, count))
    for row in range(count):
        for column in range(count):
            if row != column:
                matrix[row, column] = (
                    barycentric[column] / barycentric[row] / (points[row] - points[column])
                )
    for row in range(count):
        matrix[row, row] = -np.sum(matrix[row])
    return matrix.astype(np.float32)


def volume_matrix():
    line = lgl_derivative().astype(np.float64)
    line[0, 0] += LIFT / 2
    line[5, 5] -= LIFT / 2
    line = -2.0 * line
    eye = np.eye(6)
    whole = np.zeros((PADDED, 3 * PADDED))
    whole[:NODES, :NODES] = np.kron(np.kron(line, eye), eye)
    whole[:NODES, PADDED : PADDED + NODES] = np.kron(np.kron(eye, line), eye)
    whole[:NODES, 2 * PADDED : 2 * PADDED + NODES] = np.kron(np.kron(eye, eye), line)
    whole = whole.astype(np.float32)
    high = whole.astype(jnp.bfloat16)
    low = (whole - high.astype(np.float32)).astype(jnp.bfloat16)
    return np.stack([high, low])


def root(x):
    return x * lax.rsqrt(jnp.maximum(x, 1e-30))


def primitives(u):
    inverse = 1.0 / u[0]
    velocity = [u[1] * inverse, u[2] * inverse, u[3] * inverse]
    kinetic = u[1] * velocity[0] + u[2] * velocity[1] + u[3] * velocity[2]
    squares = [u[5] * u[5], u[6] * u[6], u[7] * u[7]]
    field_sq = squares[0] + squares[1] + squares[2]
    pressure = (GAMMA - 1.0) * (u[4] - 0.5 * (kinetic + field_sq + u[8] * u[8]))
    return inverse, velocity, squares, field_sq, pressure


def fast_terms(prims):
    _, _, _, field_sq, pressure = prims
    acoustic = GAMMA * pressure
    gap = acoustic - field_sq
    return acoustic + field_sq, gap * gap, 4.0 * acoustic


def speed_along(prims, terms, d):
    inverse, velocity, squares, _, _ = prims
    both, gap_sq, acoustic4 = terms
    across = squares[(d + 1) % 3] + squares[(d + 2) % 3]
    inner = both + root(gap_sq + acoustic4 * across)
    return jnp.maximum(jnp.abs(velocity[d]) + root(0.5 * inverse * inner), GLM_SPEED)


def face_side(u, d):
    prims = primitives(u)
    _, velocity, _, field_sq, pressure = prims
    field = u[5:8]
    total = pressure + 0.5 * field_sq
    v, b = velocity[d], field[d]
    dot = velocity[0] * field[0] + velocity[1] * field[1] + velocity[2] * field[2]
    twice = GLM_SPEED * u[8]
    flux = [u[1 + d]]
    for c in range(3):
        entry = u[1 + c] * v - field[c] * b
        flux.append(entry + total if c == d else entry)
    flux.append(v * (u[4] + total) + b * (twice - dot))
    for c in range(3):
        flux.append(twice if c == d else v * field[c] - b * velocity[c])
    flux.append(GLM_SPEED * b)
    return flux, speed_along(prims, fast_terms(prims), d)


def face_flux(left, right, d):
    left_flux, left_speed = face_side(left, d)
    right_flux, right_speed = face_side(right, d)
    half = LIFT / 2
    largest = half * jnp.maximum(left_speed, right_speed)
    return [
        half * (left_flux[c] + right_flux[c]) - largest * (right[c] - left[c]) for c in range(9)
    ]


def inflow_value(c, d, outward):
    if c == 0:
        return 1.0
    if c == 1 + d:
        return -outward * JET_SPEED
    if c == 4:
        return 1.0 / (GAMMA - 1.0) + 0.5 * JET_SPEED**2 + 0.5 * BRAKE_FIELD**2
    if c == 7:
        return BRAKE_FIELD
    return 0.0


def with_outer(inner, interior, code, d, outward):
    states = []
    for c in range(9):
        x = interior[c]
        if c == 1 + d:
            x = jnp.where(code == 1, -x, x)
        x = jnp.where(code == 0, inflow_value(c, d, outward), x)
        states.append(x if inner is None else jnp.where(code < 3, x, inner[c]))
    return states


CHUNKS = ((0, 16), (16, 16), (32, 4))


def kernel(
    nlen,
    nwid,
    u_hbm,
    mat_hbm,
    ends_hbm,
    sides_hbm,
    walls_hbm,
    out_ref,
    dt_ref,
    ends_ref,
    sides_ref,
    walls_ref,
    u0,
    u1,
    u2,
    mat,
    fhi,
    flo,
    acc,
    above,
    below,
    own_low,
    own_high,
    wide_below,
    wide_above,
    acc_low,
    acc_high,
    ghost_low,
    ghost_high,
    e_low,
    e_high,
    t_low,
    t_high,
    a_low,
    a_high,
    g_wide,
    peak,
    peak_group,
    peak_all,
    load_sem,
    send_sem,
    recv_sem,
    peak_send,
    peak_recv,
):
    li = lax.axis_index("len")
    wi = lax.axis_index("wid")
    group = max(nlen // 2, 1)
    blocks = nlen // group
    crowd = blocks * nwid
    lanes = lax.broadcasted_iota(jnp.int32, (1, LANES), 1)
    states = (u0, u1, u2, out_ref)

    load_u = pltpu.make_async_copy(u_hbm, u0.at[:, pl.ds(0, NODES), :], load_sem.at[0])
    load_m = pltpu.make_async_copy(mat_hbm, mat, load_sem.at[1])
    load_u.start()
    load_kinds = [
        pltpu.make_async_copy(src, dst, load_sem.at[2 + n])
        for n, (src, dst) in enumerate(
            ((ends_hbm, ends_ref), (sides_hbm, sides_ref), (walls_hbm, walls_ref))
        )
    ]
    for load in load_kinds:
        load.start()
    load_m.start()

    in_group = lax.rem(li, group)
    block = li // group
    base = block * group
    in_crowd = block * nwid + wi

    def group_peer(step):
        return (base + lax.rem(in_group + step, group), wi)

    def crowd_peer(step):
        other = lax.rem(in_crowd + step, crowd)
        return ((other // nwid) * group + in_group, lax.rem(other, nwid))

    barrier = pltpu.get_barrier_semaphore()

    def greet(peer):
        pl.semaphore_signal(barrier, inc=1, device_id=peer, device_id_type=MESH)

    has_prev, has_next = li > 0, li < nlen - 1
    has_left, has_right = wi > 0, wi < nwid - 1

    for step in range(1, crowd // 2 + 1):
        greet(crowd_peer(step))
        if step < crowd - step:
            greet(crowd_peer(crowd - step))

    @pl.when(has_prev)
    def _():
        greet((li - 1, wi))

    @pl.when(has_next)
    def _():
        greet((li + 1, wi))

    @pl.loop(1, group)
    def _(step):
        greet(group_peer(step))

    for ref in states[:3]:
        for c in range(9):
            ref[c, pl.ds(NODES, 8), :] = jnp.ones((8, LANES), jnp.float32)

    z = lanes % EZ
    y = lanes // EZ
    wide = LANES // EZ

    def tiled(row):
        return jnp.concatenate([row] * wide, axis=1)

    def wall_row(side):
        row = walls_ref[side]
        parts = [jnp.broadcast_to(row[:, q : q + 1], (1, EZ)) for q in range(wide)]
        return jnp.concatenate(parts, axis=1)

    def ends_row(side):
        return jnp.concatenate([ends_ref[side, q : q + 1, :] for q in range(wide)], axis=1)


    def copy_prev(s):
        return pltpu.make_async_remote_copy(
            src_ref=states[s].at[:, pl.ds(0, HALO), :],
            dst_ref=above.at[s],
            send_sem=send_sem.at[s, 0],
            recv_sem=recv_sem.at[s, 0],
            device_id=(li - 1, wi),
            device_id_type=MESH,
        )

    def copy_next(s):
        return pltpu.make_async_remote_copy(
            src_ref=states[s].at[:, pl.ds(NODES - HALO, HALO), :],
            dst_ref=below.at[s],
            send_sem=send_sem.at[s, 1],
            recv_sem=recv_sem.at[s, 1],
            device_id=(li + 1, wi),
            device_id_type=MESH,
        )

    def copy_left(s):
        return pltpu.make_async_remote_copy(
            src_ref=own_low.at[0] if s == 0 else acc_low.at[s - 1],
            dst_ref=wide_above.at[s],
            send_sem=send_sem.at[s, 2],
            recv_sem=recv_sem.at[s, 2],
            device_id=(li, wi - 1),
            device_id_type=MESH,
        )

    def copy_right(s):
        return pltpu.make_async_remote_copy(
            src_ref=own_high.at[0] if s == 0 else acc_high.at[s - 1],
            dst_ref=wide_below.at[s],
            send_sem=send_sem.at[s, 3],
            recv_sem=recv_sem.at[s, 3],
            device_id=(li, wi + 1),
            device_id_type=MESH,
        )

    def roll(x, by):
        by = by % LANES
        return x if by == 0 else pltpu.roll(x, by, axis=1)

    def packed(ref):
        return [ref[pl.ds(c, PACK, stride=9), :] for c in range(9)]

    def send_width(s):
        @pl.when(has_left)
        def _():
            copy_left(s).start()

        @pl.when(has_right)
        def _():
            copy_right(s).start()

    def send_length(s):
        @pl.when(has_prev)
        def _():
            copy_prev(s).start()

        @pl.when(has_next)
        def _():
            copy_next(s).start()

    def traces(ref, low, high):
        for c in range(9):
            for i in range(6):
                low[c, pl.ds(6 * i, 6), :] = ref[c, pl.ds(36 * i, 6), :]
                high[c, pl.ds(6 * i, 6), :] = ref[c, pl.ds(36 * i + 30, 6), :]

    def pack(ref, dest, slot, first):
        for c in range(9):
            whole = None
            for q in range(wide):
                piece = roll(ref[c, pl.ds(q, PACK, stride=4), :], EZ * (q - first))
                whole = piece if q == 0 else jnp.where(y == q, piece, whole)
            dest[slot, pl.ds(c, PACK, stride=9), :] = whole

    def pack_width(s):
        traces(acc, a_low, a_high)
        pack(a_low, acc_low, s, 0)
        pack(a_high, acc_high, s, wide - 1)

    def scatter(s):
        u = states[s]
        for ref, src, first in ((t_low, own_low, 0), (t_high, own_high, wide - 1)):
            for c in range(9):
                new = src[s, pl.ds(c, PACK, stride=9), :]
                for q in range(wide):
                    rows = pl.ds(q, PACK, stride=4)
                    ref[c, rows, :] = jnp.where(
                        y == first, roll(new, EZ * (first - q)), ref[c, rows, :]
                    )
        for c in range(9):
            for i in range(6):
                u[c, pl.ds(36 * i, 6), :] = t_low[c, pl.ds(6 * i, 6), :]
                u[c, pl.ds(36 * i + 30, 6), :] = t_high[c, pl.ds(6 * i, 6), :]

    def volume(s):
        u_ref = states[s]

        def put(d, c, parts):
            fhi[pl.ds(rows[d], 16), pl.ds(c * LANES, LANES)] = parts[0]
            flo[pl.ds(rows[d], 16), pl.ds(c * LANES, LANES)] = parts[1]

        def split(x):
            high = x.astype(jnp.bfloat16)
            return high, (x - high.astype(jnp.float32)).astype(jnp.bfloat16)

        rows = [None] * 3

        def body(chunk, _):
            start = pl.multiple_of(chunk * 16, 16)
            for d in range(3):
                rows[d] = pl.multiple_of(d * PADDED + chunk * 16, 16)
            u = [u_ref[c, pl.ds(start, 16), :] for c in range(9)]
            prims = primitives(u)
            _, velocity, _, field_sq, pressure = prims
            field = u[5:8]
            total = pressure + 0.5 * field_sq
            enthalpy = u[4] + total
            twice = GLM_SPEED * u[8]
            back = twice - (
                velocity[0] * field[0] + velocity[1] * field[1] + velocity[2] * field[2]
            )
            psi_parts = split(twice)
            for d in range(3):
                put(d, 0, split(u[1 + d]))
                put(d, 5 + d, psi_parts)
                put(d, 8, split(GLM_SPEED * field[d]))
                put(d, 4, split(velocity[d] * enthalpy + field[d] * back))
                put(d, 1 + d, split(u[1 + d] * velocity[d] - field[d] * field[d] + total))
                for e in range(d + 1, 3):
                    shear = split(u[1 + d] * velocity[e] - field[d] * field[e])
                    put(d, 1 + e, shear)
                    put(e, 1 + d, shear)
                    turn = split(velocity[d] * field[e] - field[d] * velocity[e])
                    put(d, 5 + e, turn)
                    put(e, 5 + d, (-turn[0], -turn[1]))
            return 0

        lax.fori_loop(0, PADDED // 16, body, 0)

    def largest_speed():
        def body(chunk, top):
            start = pl.multiple_of(chunk * 8, 8)
            prims = primitives([u0[c, pl.ds(start, 8), :] for c in range(9)])
            terms = fast_terms(prims)
            for d in range(3):
                top = jnp.maximum(top, speed_along(prims, terms, d))
            return top

        start = jnp.full((8, LANES), GLM_SPEED, jnp.float32)
        top = lax.fori_loop(0, NODES // 8, body, start, unroll=3)
        peak[...] = jnp.max(top, axis=0, keepdims=True)

    def derivatives(midway=None):
        for first in range(0, 9, 2):
            if first == 4 and midway is not None:
                midway()
            count = min(2, 9 - first)
            span = pl.ds(first * LANES, count * LANES)
            high = fhi[:, span]
            result = jnp.dot(mat[0], high, preferred_element_type=jnp.float32)
            result += jnp.dot(mat[1], high, preferred_element_type=jnp.float32)
            result += jnp.dot(mat[0], flo[:, span], preferred_element_type=jnp.float32)
            for c in range(count):
                acc[first + c] = result[:, c * LANES : (c + 1) * LANES]

    def inner_faces(s, low_wall, high_wall):
        u_ref = states[s]
        for first, count in CHUNKS:
            low_rows = pl.ds(6 * first, count, stride=6)
            high_rows = pl.ds(6 * first + 5, count, stride=6)
            low = [u_ref[c, low_rows, :] for c in range(9)]
            high = [u_ref[c, high_rows, :] for c in range(9)]
            beside = [roll(x, 1) for x in high]
            left = with_outer(beside, low, low_wall, 2, -1.0)
            flux = face_flux(left, low, 2)
            for c in range(9):
                acc[c, low_rows, :] = acc[c, low_rows, :] + flux[c]
            last = face_flux(high, with_outer(None, high, high_wall, 2, 1.0), 2)
            for c in range(9):
                upper = jnp.where(z == EZ - 1, last[c], roll(flux[c], -1))
                acc[c, high_rows, :] = acc[c, high_rows, :] - upper
        for first, count in CHUNKS:
            rows = pl.ds(first, count)
            low = [t_low[c, rows, :] for c in range(9)]
            left = [roll(t_high[c, rows, :], EZ) for c in range(9)]
            flux = face_flux(left, low, 1)
            for c in range(9):
                g_wide[c, rows, :] = flux[c]
        for c in range(9):
            for i in range(6):
                flux = g_wide[c, pl.ds(6 * i, 6), :]
                rows = pl.ds(36 * i, 6)
                acc[c, rows, :] = acc[c, rows, :] + jnp.where(y > 0, flux, 0.0)
                rows = pl.ds(36 * i + 30, 6)
                acc[c, rows, :] = acc[c, rows, :] - jnp.where(y < wide - 1, roll(flux, -EZ), 0.0)

    def advance(s, step, start, current, change):
        first, own, factor = STAGES[s]
        new = own * current + (step * factor) * change
        return new + first * start if first else new

    def width_edges(s, step):
        sides = (
            (has_left, copy_right, wide_below, ghost_low, e_low, -1.0, own_low, 0),
            (has_right, copy_left, wide_above, ghost_high, e_high, 1.0, own_high, 1),
        )
        for have, copy, received, ghost, edge, sign, own, side in sides:

            @pl.when(have)
            def _(copy=copy, received=received, ghost=ghost, edge=edge, sign=sign):
                copy(s).wait_recv()
                for c in range(9):
                    rows = pl.ds(c, PACK, stride=9)
                    new = received[s, rows, :]
                    if s:
                        change = new + sign * edge[s - 1, rows, :]
                        old = ghost[s - 1, rows, :]
                        new = advance(s - 1, step, ghost[0, rows, :], old, change)
                    ghost[s, rows, :] = new

            @pl.when(jnp.logical_not(have))
            def _(ghost=ghost, own=own, side=side, sign=sign):
                outer = with_outer(None, packed(own.at[s]), tiled(sides_ref[side]), 1, sign)
                for c in range(9):
                    ghost[s, pl.ds(c, PACK, stride=9), :] = outer[c]

        low = face_flux(packed(ghost_low.at[s]), packed(own_low.at[s]), 1)
        high = face_flux(packed(own_high.at[s]), packed(ghost_high.at[s]), 1)
        for fluxes, edge, own, change, sign in (
            (low, e_low, own_low, acc_low, 1.0),
            (high, e_high, own_high, acc_high, -1.0),
        ):
            for c in range(9):
                rows = pl.ds(c, PACK, stride=9)
                edge[s, rows, :] = fluxes[c]
                own[s + 1, rows, :] = advance(
                    s,
                    step,
                    own[0, rows, :],
                    own[s, rows, :],
                    change[s, rows, :] + sign * fluxes[c],
                )

    def length_edges(s):
        u_ref = states[s]
        top = NODES - FACE
        skip = HALO - FACE

        @pl.when(has_prev)
        def _():
            copy_next(s).wait_recv()

        @pl.when(has_next)
        def _():
            copy_prev(s).wait_recv()

        @pl.when(jnp.logical_not(has_prev))
        def _():
            for first, count in CHUNKS:
                own = [u_ref[c, pl.ds(first, count), :] for c in range(9)]
                outer = with_outer(None, own, ends_row(0), 0, -1.0)
                for c in range(9):
                    below[s, c, pl.ds(skip + first, count), :] = outer[c]

        @pl.when(jnp.logical_not(has_next))
        def _():
            for first, count in CHUNKS:
                own = [u_ref[c, pl.ds(top + first, count), :] for c in range(9)]
                outer = with_outer(None, own, ends_row(1), 0, 1.0)
                for c in range(9):
                    above[s, c, pl.ds(first, count), :] = outer[c]

        for first, count in CHUNKS:
            rows = pl.ds(first, count)
            left = [below[s, c, pl.ds(skip + first, count), :] for c in range(9)]
            flux = face_flux(left, [u_ref[c, rows, :] for c in range(9)], 0)
            for c in range(9):
                acc[c, rows, :] = acc[c, rows, :] + flux[c]
        for first, count in CHUNKS:
            rows = pl.ds(top + first, count)
            right = [above[s, c, pl.ds(first, count), :] for c in range(9)]
            flux = face_flux([u_ref[c, rows, :] for c in range(9)], right, 0)
            for c in range(9):
                acc[c, rows, :] = acc[c, rows, :] - flux[c]

    def update(s, step, spans):
        first, own, factor = STAGES[s]
        weight = step * factor
        for start, count in spans:
            for c in range(9):
                rows = pl.ds(start, count)
                new = own * states[s][c, rows, :] + weight * acc[c, rows, :]
                if first:
                    new = new + first * u0[c, rows, :]
                states[s + 1][c, rows, :] = new

    def peak_copy(src, dst, which, step, peer):
        return pltpu.make_async_remote_copy(
            src_ref=src,
            dst_ref=dst.at[step - 1],
            send_sem=peak_send.at[which],
            recv_sem=peak_recv.at[which],
            device_id=peer,
            device_id_type=MESH,
        )

    inner_rows = ((HALO, NODES - 2 * HALO),)
    outer_rows = ((0, HALO), (NODES - HALO, HALO))

    def second_round():
        pltpu.make_async_copy(peak_group, peak_group, peak_recv.at[0]).wait()
        pltpu.make_async_copy(peak_group, peak_group, peak_send.at[0]).wait()
        peak[...] = jnp.maximum(peak[...], jnp.max(peak_group[...], axis=0))

        @pl.loop(1, crowd)
        def _(step):
            peak_copy(peak, peak_all, 1, step, crowd_peer(step)).start()

    load_u.wait()
    largest_speed()
    traces(u0, t_low, t_high)
    pack(t_low, own_low, 0, 0)
    pack(t_high, own_high, 0, wide - 1)
    for load in load_kinds:
        load.wait()
    low_wall = jnp.where(z == 0, wall_row(0), 3)
    high_wall = wall_row(1)
    neighbours = has_prev.astype(jnp.int32) + has_next.astype(jnp.int32)
    pl.semaphore_wait(barrier, group - 1 + crowd - 1 + neighbours)
    send_width(0)

    @pl.loop(1, group)
    def _(step):
        peak_copy(peak, peak_group, 0, step, group_peer(step)).start()

    step_row = None
    for s in range(3):
        send_length(s)
        volume(s)
        if s == 0:
            load_m.wait()
        derivatives(second_round if s == 0 else None)
        inner_faces(s, low_wall, high_wall)
        if s:
            update(s, step_row, inner_rows)
        length_edges(s)
        pack_width(s)
        if s < 2:
            send_width(s + 1)
        if s == 0:
            pltpu.make_async_copy(peak_all, peak_all, peak_recv.at[1]).wait()
            fastest = jnp.maximum(peak[...], jnp.max(peak_all[...], axis=0))
            fastest = jnp.max(fastest, axis=1, keepdims=True)
            step_row = CFL_NUMBER / (11.0 * jnp.broadcast_to(fastest, (1, LANES)))
            dt_ref[0, 0] = jnp.max(step_row)
            update(s, step_row, inner_rows)
        update(s, step_row, outer_rows)
        traces(states[s + 1], t_low, t_high)
        width_edges(s, step_row)
        scatter(s + 1)

    pltpu.make_async_copy(peak_all, peak_all, peak_send.at[1]).wait()
    for s in range(3):
        for have, copy in (
            (has_prev, copy_prev),
            (has_next, copy_next),
            (has_left, copy_left),
            (has_right, copy_right),
        ):

            @pl.when(have)
            def _(copy=copy):
                copy(s).wait_send()


def solution(mesh):
    nlen, nwid = mesh.shape["len"], mesh.shape["wid"]
    group = max(nlen // 2, 1)
    crowd = nlen // group * nwid
    matrix = volume_matrix()

    def on_device(conserved, ends_kind, sides_kind, walls_kind):
        f32 = jnp.float32
        vmem = pl.BlockSpec(memory_space=pltpu.VMEM)
        hbm = pl.BlockSpec(memory_space=pl.ANY)
        state = pltpu.VMEM((9, PADDED, LANES), f32)
        halo = pltpu.VMEM((3, 9, HALO, LANES), f32)
        pack = pltpu.VMEM((3, 9 * PACK, LANES), f32)
        own_pack = pltpu.VMEM((4, 9 * PACK, LANES), f32)
        trace = pltpu.VMEM((9, HALO, LANES), f32)
        flux = pltpu.VMEM((3 * PADDED, 9 * LANES), jnp.bfloat16)
        updated, step = pl.pallas_call(
            functools.partial(kernel, nlen, nwid),
            out_shape=(
                jax.ShapeDtypeStruct((9, NODES, LANES), f32),
                jax.ShapeDtypeStruct((1, 1), f32),
            ),
            in_specs=[hbm] * 5,
            out_specs=(vmem, pl.BlockSpec(memory_space=pltpu.SMEM)),
            scratch_shapes=[
                pltpu.VMEM((2, LANES // EZ, EZ), jnp.int32),
                pltpu.VMEM((2, 1, EZ), jnp.int32),
                pltpu.VMEM((2, 1, LANES // EZ), jnp.int32),
                state,
                state,
                state,
                pltpu.VMEM((2, PADDED, 3 * PADDED), jnp.bfloat16),
                flux,
                flux,
                state,
                halo,
                halo,
                own_pack,
                own_pack,
                pack,
                pack,
                pack,
                pack,
                pack,
                pack,
                pack,
                pack,
                trace,
                trace,
                trace,
                trace,
                trace,
                pltpu.VMEM((1, LANES), f32),
                pltpu.VMEM((max(group - 1, 1), 1, LANES), f32),
                pltpu.VMEM((max(crowd - 1, 1), 1, LANES), f32),
                pltpu.SemaphoreType.DMA((5,)),
                pltpu.SemaphoreType.DMA((3, 4)),
                pltpu.SemaphoreType.DMA((3, 4)),
                pltpu.SemaphoreType.DMA((2,)),
                pltpu.SemaphoreType.DMA((2,)),
            ],
            compiler_params=pltpu.CompilerParams(
                collective_id=0, has_side_effects=True, vmem_limit_bytes=40 * 1024 * 1024
            ),
        )(
            *(
                pltpu.with_memory_space_constraint(x, pltpu.HBM)
                for x in (
                    conserved.reshape(9, NODES, LANES),
                    jnp.asarray(matrix),
                    ends_kind,
                    sides_kind,
                    walls_kind,
                )
            )
        )
        return updated.reshape(conserved.shape), step.reshape(())

    return jax.shard_map(
        on_device,
        mesh=mesh,
        in_specs=(
            P(None, None, None, None, "len", "wid"),
            P(None, "wid", None),
            P(None, "len", None),
            P(None, "len", "wid"),
        ),
        out_specs=(P(None, None, None, None, "len", "wid"), P()),
        check_vma=False,
    )
```

```python
import functools

import jax
import jax.numpy as jnp
import numpy as np
from jax import lax
from jax.experimental import pallas as pl
from jax.experimental.pallas import tpu as pltpu
from jax.sharding import PartitionSpec as P

MESH = pl.DeviceIdType.MESH

EZ = 32
LANES = 128
NODES = 216
PADDED = 224
FACE = 36
HALO = 40
PACK = 9

GAMMA = 5.0 / 3.0
GLM_SPEED = 2.0
JET_SPEED = 0.8
BRAKE_FIELD = 1.0
CFL_NUMBER = 0.1
LIFT = 30.0

STAGES = ((0.0, 1.0, 1.0), (0.75, 0.25, 0.25), (1.0 / 3.0, 2.0 / 3.0, 2.0 / 3.0))


def lgl_derivative():
    points = np.array(
        [
            -1.0,
            -0.7650553239294647,
            -0.2852315164806451,
            0.2852315164806451,
            0.7650553239294647,
            1.0,
        ]
    )
    count = points.shape[0]
    barycentric = np.ones(count)
    for row in range(count):
        for column in range(count):
            if row != column:
                barycentric[row] = barycentric[row] / (points[row] - points[column])
    matrix = np.zeros((count, count))
    for row in range(count):
        for column in range(count):
            if row != column:
                matrix[row, column] = (
                    barycentric[column] / barycentric[row] / (points[row] - points[column])
                )
    for row in range(count):
        matrix[row, row] = -np.sum(matrix[row])
    return matrix.astype(np.float32)


def volume_matrix():
    line = lgl_derivative().astype(np.float64)
    line[0, 0] += LIFT / 2
    line[5, 5] -= LIFT / 2
    line = -2.0 * line
    eye = np.eye(6)
    whole = np.zeros((PADDED, 3 * PADDED))
    whole[:NODES, :NODES] = np.kron(np.kron(line, eye), eye)
    whole[:NODES, PADDED : PADDED + NODES] = np.kron(np.kron(eye, line), eye)
    whole[:NODES, 2 * PADDED : 2 * PADDED + NODES] = np.kron(np.kron(eye, eye), line)
    whole = whole.astype(np.float32)
    high = whole.astype(jnp.bfloat16)
    low = (whole - high.astype(np.float32)).astype(jnp.bfloat16)
    return np.stack([high, low])


def peak_rounds(nlen, nwid):
    near = min(8, nlen)
    return near, nwid // 2, nlen // near * 2


def root(x):
    return x * lax.rsqrt(jnp.maximum(x, 1e-30))


def primitives(u):
    inverse = 1.0 / u[0]
    velocity = [u[1] * inverse, u[2] * inverse, u[3] * inverse]
    kinetic = u[1] * velocity[0] + u[2] * velocity[1] + u[3] * velocity[2]
    squares = [u[5] * u[5], u[6] * u[6], u[7] * u[7]]
    field_sq = squares[0] + squares[1] + squares[2]
    pressure = (GAMMA - 1.0) * (u[4] - 0.5 * (kinetic + field_sq + u[8] * u[8]))
    return inverse, velocity, squares, field_sq, pressure


def fast_terms(prims):
    _, _, _, field_sq, pressure = prims
    acoustic = GAMMA * pressure
    gap = acoustic - field_sq
    return acoustic + field_sq, gap * gap, 4.0 * acoustic


def speed_along(prims, terms, d):
    inverse, velocity, squares, _, _ = prims
    both, gap_sq, acoustic4 = terms
    across = squares[(d + 1) % 3] + squares[(d + 2) % 3]
    inner = both + root(gap_sq + acoustic4 * across)
    return jnp.maximum(jnp.abs(velocity[d]) + root(0.5 * inverse * inner), GLM_SPEED)


def face_side(u, d):
    prims = primitives(u)
    _, velocity, _, field_sq, pressure = prims
    field = u[5:8]
    total = pressure + 0.5 * field_sq
    v, b = velocity[d], field[d]
    dot = velocity[0] * field[0] + velocity[1] * field[1] + velocity[2] * field[2]
    twice = GLM_SPEED * u[8]
    flux = [u[1 + d]]
    for c in range(3):
        entry = u[1 + c] * v - field[c] * b
        flux.append(entry + total if c == d else entry)
    flux.append(v * (u[4] + total) + b * (twice - dot))
    for c in range(3):
        flux.append(twice if c == d else v * field[c] - b * velocity[c])
    flux.append(GLM_SPEED * b)
    return flux, speed_along(prims, fast_terms(prims), d)


def face_flux(left, right, d):
    left_flux, left_speed = face_side(left, d)
    right_flux, right_speed = face_side(right, d)
    half = LIFT / 2
    largest = half * jnp.maximum(left_speed, right_speed)
    return [
        half * (left_flux[c] + right_flux[c]) - largest * (right[c] - left[c]) for c in range(9)
    ]


def inflow_value(c, d, outward):
    if c == 0:
        return 1.0
    if c == 1 + d:
        return -outward * JET_SPEED
    if c == 4:
        return 1.0 / (GAMMA - 1.0) + 0.5 * JET_SPEED**2 + 0.5 * BRAKE_FIELD**2
    if c == 7:
        return BRAKE_FIELD
    return 0.0


def with_outer(inner, interior, code, d, outward):
    states = []
    for c in range(9):
        x = interior[c]
        if c == 1 + d:
            x = jnp.where(code == 1, -x, x)
        x = jnp.where(code == 0, inflow_value(c, d, outward), x)
        states.append(x if inner is None else jnp.where(code < 3, x, inner[c]))
    return states


CHUNKS = ((0, 16), (16, 16), (32, 4))


def kernel(
    nlen,
    nwid,
    u_hbm,
    mat_hbm,
    ends_hbm,
    sides_hbm,
    walls_hbm,
    out_ref,
    dt_ref,
    ends_ref,
    sides_ref,
    walls_ref,
    u0,
    u1,
    u2,
    mat,
    fhi,
    flo,
    acc,
    above,
    below,
    own_low,
    own_high,
    wide_below,
    wide_above,
    acc_low,
    acc_high,
    ghost_low,
    ghost_high,
    e_low,
    e_high,
    t_low,
    t_high,
    a_low,
    a_high,
    g_wide,
    peak,
    peaks0,
    peaks1,
    peaks2,
    load_sem,
    send_sem,
    recv_sem,
    peak_send,
    peak_recv,
):
    li = lax.axis_index("len")
    wi = lax.axis_index("wid")
    rounds = peak_rounds(nlen, nwid)
    near, rows_of_chips, columns = rounds
    lanes = lax.broadcasted_iota(jnp.int32, (1, LANES), 1)
    states = (u0, u1, u2, out_ref)
    peaks = (peaks0, peaks1, peaks2)

    load_u = pltpu.make_async_copy(u_hbm, u0.at[:, pl.ds(0, NODES), :], load_sem.at[0])
    load_m = pltpu.make_async_copy(mat_hbm, mat, load_sem.at[1])
    load_u.start()
    load_kinds = [
        pltpu.make_async_copy(src, dst, load_sem.at[2 + n])
        for n, (src, dst) in enumerate(
            ((ends_hbm, ends_ref), (sides_hbm, sides_ref), (walls_hbm, walls_ref))
        )
    ]
    for load in load_kinds:
        load.start()
    load_m.start()

    in_near, block = lax.rem(li, near), li // near
    in_column, row = lax.rem(wi, 2), wi // 2
    in_columns = block * 2 + in_column

    def peer(which, step):
        if which == 0:
            return (block * near + lax.rem(in_near + step, near), wi)
        if which == 1:
            return (li, lax.rem(row + step, rows_of_chips) * 2 + in_column)
        other = lax.rem(in_columns + step, columns)
        return ((other // 2) * near + in_near, row * 2 + lax.rem(other, 2))

    barrier = pltpu.get_barrier_semaphore()

    def greet(device):
        pl.semaphore_signal(barrier, inc=1, device_id=device, device_id_type=MESH)

    has_prev, has_next = li > 0, li < nlen - 1
    has_left, has_right = wi > 0, wi < nwid - 1

    for have, device in (
        (has_left, (li, wi - 1)),
        (has_right, (li, wi + 1)),
        (has_prev, (li - 1, wi)),
        (has_next, (li + 1, wi)),
    ):

        @pl.when(have)
        def _(device=device):
            greet(device)

    for which in (2, 1, 0):
        for step in range(1, rounds[which]):
            greet(peer(which, step))

    for ref in states[:3]:
        for c in range(9):
            ref[c, pl.ds(NODES, 8), :] = jnp.ones((8, LANES), jnp.float32)

    z = lanes % EZ
    y = lanes // EZ
    wide = LANES // EZ

    def tiled(row):
        return jnp.concatenate([row] * wide, axis=1)

    def wall_row(side):
        row = walls_ref[side]
        parts = [jnp.broadcast_to(row[:, q : q + 1], (1, EZ)) for q in range(wide)]
        return jnp.concatenate(parts, axis=1)

    def ends_row(side):
        return jnp.concatenate([ends_ref[side, q : q + 1, :] for q in range(wide)], axis=1)


    def copy_prev(s):
        return pltpu.make_async_remote_copy(
            src_ref=states[s].at[:, pl.ds(0, HALO), :],
            dst_ref=above.at[s],
            send_sem=send_sem.at[s, 0],
            recv_sem=recv_sem.at[s, 0],
            device_id=(li - 1, wi),
            device_id_type=MESH,
        )

    def copy_next(s):
        return pltpu.make_async_remote_copy(
            src_ref=states[s].at[:, pl.ds(NODES - HALO, HALO), :],
            dst_ref=below.at[s],
            send_sem=send_sem.at[s, 1],
            recv_sem=recv_sem.at[s, 1],
            device_id=(li + 1, wi),
            device_id_type=MESH,
        )

    def copy_left(s):
        return pltpu.make_async_remote_copy(
            src_ref=own_low.at[0] if s == 0 else acc_low.at[s - 1],
            dst_ref=wide_above.at[s],
            send_sem=send_sem.at[s, 2],
            recv_sem=recv_sem.at[s, 2],
            device_id=(li, wi - 1),
            device_id_type=MESH,
        )

    def copy_right(s):
        return pltpu.make_async_remote_copy(
            src_ref=own_high.at[0] if s == 0 else acc_high.at[s - 1],
            dst_ref=wide_below.at[s],
            send_sem=send_sem.at[s, 3],
            recv_sem=recv_sem.at[s, 3],
            device_id=(li, wi + 1),
            device_id_type=MESH,
        )

    def roll(x, by):
        by = by % LANES
        return x if by == 0 else pltpu.roll(x, by, axis=1)

    def packed(ref):
        return [ref[pl.ds(c, PACK, stride=9), :] for c in range(9)]

    def send_width(s):
        @pl.when(has_left)
        def _():
            copy_left(s).start()

        @pl.when(has_right)
        def _():
            copy_right(s).start()

    def send_length(s):
        @pl.when(has_prev)
        def _():
            copy_prev(s).start()

        @pl.when(has_next)
        def _():
            copy_next(s).start()

    def traces(ref, low, high):
        for c in range(9):
            for i in range(6):
                low[c, pl.ds(6 * i, 6), :] = ref[c, pl.ds(36 * i, 6), :]
                high[c, pl.ds(6 * i, 6), :] = ref[c, pl.ds(36 * i + 30, 6), :]

    def pack(ref, dest, slot, first):
        for c in range(9):
            whole = None
            for q in range(wide):
                piece = roll(ref[c, pl.ds(q, PACK, stride=4), :], EZ * (q - first))
                whole = piece if q == 0 else jnp.where(y == q, piece, whole)
            dest[slot, pl.ds(c, PACK, stride=9), :] = whole

    def pack_width(s):
        traces(acc, a_low, a_high)
        pack(a_low, acc_low, s, 0)
        pack(a_high, acc_high, s, wide - 1)

    def scatter(s):
        u = states[s]
        for ref, src, first in ((t_low, own_low, 0), (t_high, own_high, wide - 1)):
            for c in range(9):
                new = src[s, pl.ds(c, PACK, stride=9), :]
                for q in range(wide):
                    rows = pl.ds(q, PACK, stride=4)
                    ref[c, rows, :] = jnp.where(
                        y == first, roll(new, EZ * (first - q)), ref[c, rows, :]
                    )
        for c in range(9):
            for i in range(6):
                u[c, pl.ds(36 * i, 6), :] = t_low[c, pl.ds(6 * i, 6), :]
                u[c, pl.ds(36 * i + 30, 6), :] = t_high[c, pl.ds(6 * i, 6), :]

    def volume(s):
        u_ref = states[s]

        def put(d, c, parts):
            fhi[pl.ds(rows[d], 16), pl.ds(c * LANES, LANES)] = parts[0]
            flo[pl.ds(rows[d], 16), pl.ds(c * LANES, LANES)] = parts[1]

        def split(x):
            high = x.astype(jnp.bfloat16)
            return high, (x - high.astype(jnp.float32)).astype(jnp.bfloat16)

        rows = [None] * 3

        def body(chunk, _):
            start = pl.multiple_of(chunk * 16, 16)
            for d in range(3):
                rows[d] = pl.multiple_of(d * PADDED + chunk * 16, 16)
            u = [u_ref[c, pl.ds(start, 16), :] for c in range(9)]
            prims = primitives(u)
            _, velocity, _, field_sq, pressure = prims
            field = u[5:8]
            total = pressure + 0.5 * field_sq
            enthalpy = u[4] + total
            twice = GLM_SPEED * u[8]
            back = twice - (
                velocity[0] * field[0] + velocity[1] * field[1] + velocity[2] * field[2]
            )
            psi_parts = split(twice)
            for d in range(3):
                put(d, 0, split(u[1 + d]))
                put(d, 5 + d, psi_parts)
                put(d, 8, split(GLM_SPEED * field[d]))
                put(d, 4, split(velocity[d] * enthalpy + field[d] * back))
                put(d, 1 + d, split(u[1 + d] * velocity[d] - field[d] * field[d] + total))
                for e in range(d + 1, 3):
                    shear = split(u[1 + d] * velocity[e] - field[d] * field[e])
                    put(d, 1 + e, shear)
                    put(e, 1 + d, shear)
                    turn = split(velocity[d] * field[e] - field[d] * velocity[e])
                    put(d, 5 + e, turn)
                    put(e, 5 + d, (-turn[0], -turn[1]))
            return 0

        lax.fori_loop(0, PADDED // 16, body, 0)

    def largest_speed():
        def body(chunk, top):
            start = pl.multiple_of(chunk * 8, 8)
            prims = primitives([u0[c, pl.ds(start, 8), :] for c in range(9)])
            terms = fast_terms(prims)
            for d in range(3):
                top = jnp.maximum(top, speed_along(prims, terms, d))
            return top

        start = jnp.full((8, LANES), GLM_SPEED, jnp.float32)
        top = lax.fori_loop(0, NODES // 8, body, start, unroll=3)
        peak[0] = jnp.max(top, axis=0, keepdims=True)

    def derivatives(midway=None):
        for first in range(0, 9, 2):
            if first == 4 and midway is not None:
                midway()
            count = min(2, 9 - first)
            span = pl.ds(first * LANES, count * LANES)
            high = fhi[:, span]
            result = jnp.dot(mat[0], high, preferred_element_type=jnp.float32)
            result += jnp.dot(mat[1], high, preferred_element_type=jnp.float32)
            result += jnp.dot(mat[0], flo[:, span], preferred_element_type=jnp.float32)
            for c in range(count):
                acc[first + c] = result[:, c * LANES : (c + 1) * LANES]

    def inner_faces(s, low_wall, high_wall):
        u_ref = states[s]
        for first, count in CHUNKS:
            low_rows = pl.ds(6 * first, count, stride=6)
            high_rows = pl.ds(6 * first + 5, count, stride=6)
            low = [u_ref[c, low_rows, :] for c in range(9)]
            high = [u_ref[c, high_rows, :] for c in range(9)]
            beside = [roll(x, 1) for x in high]
            left = with_outer(beside, low, low_wall, 2, -1.0)
            flux = face_flux(left, low, 2)
            for c in range(9):
                acc[c, low_rows, :] = acc[c, low_rows, :] + flux[c]
            last = face_flux(high, with_outer(None, high, high_wall, 2, 1.0), 2)
            for c in range(9):
                upper = jnp.where(z == EZ - 1, last[c], roll(flux[c], -1))
                acc[c, high_rows, :] = acc[c, high_rows, :] - upper
        for first, count in CHUNKS:
            rows = pl.ds(first, count)
            low = [t_low[c, rows, :] for c in range(9)]
            left = [roll(t_high[c, rows, :], EZ) for c in range(9)]
            flux = face_flux(left, low, 1)
            for c in range(9):
                g_wide[c, rows, :] = flux[c]
        for c in range(9):
            for i in range(6):
                flux = g_wide[c, pl.ds(6 * i, 6), :]
                rows = pl.ds(36 * i, 6)
                acc[c, rows, :] = acc[c, rows, :] + jnp.where(y > 0, flux, 0.0)
                rows = pl.ds(36 * i + 30, 6)
                acc[c, rows, :] = acc[c, rows, :] - jnp.where(y < wide - 1, roll(flux, -EZ), 0.0)

    def advance(s, step, start, current, change):
        first, own, factor = STAGES[s]
        new = own * current + (step * factor) * change
        return new + first * start if first else new

    def width_edges(s, step):
        sides = (
            (has_left, copy_right, wide_below, ghost_low, e_low, -1.0, own_low, 0),
            (has_right, copy_left, wide_above, ghost_high, e_high, 1.0, own_high, 1),
        )
        for have, copy, received, ghost, edge, sign, own, side in sides:

            @pl.when(have)
            def _(copy=copy, received=received, ghost=ghost, edge=edge, sign=sign):
                copy(s).wait_recv()
                for c in range(9):
                    rows = pl.ds(c, PACK, stride=9)
                    new = received[s, rows, :]
                    if s:
                        change = new + sign * edge[s - 1, rows, :]
                        old = ghost[s - 1, rows, :]
                        new = advance(s - 1, step, ghost[0, rows, :], old, change)
                    ghost[s, rows, :] = new

            @pl.when(jnp.logical_not(have))
            def _(ghost=ghost, own=own, side=side, sign=sign):
                outer = with_outer(None, packed(own.at[s]), tiled(sides_ref[side]), 1, sign)
                for c in range(9):
                    ghost[s, pl.ds(c, PACK, stride=9), :] = outer[c]

        low = face_flux(packed(ghost_low.at[s]), packed(own_low.at[s]), 1)
        high = face_flux(packed(own_high.at[s]), packed(ghost_high.at[s]), 1)
        for fluxes, edge, own, change, sign in (
            (low, e_low, own_low, acc_low, 1.0),
            (high, e_high, own_high, acc_high, -1.0),
        ):
            for c in range(9):
                rows = pl.ds(c, PACK, stride=9)
                edge[s, rows, :] = fluxes[c]
                own[s + 1, rows, :] = advance(
                    s,
                    step,
                    own[0, rows, :],
                    own[s, rows, :],
                    change[s, rows, :] + sign * fluxes[c],
                )

    def length_edges(s):
        u_ref = states[s]
        top = NODES - FACE
        skip = HALO - FACE

        @pl.when(has_prev)
        def _():
            copy_next(s).wait_recv()

        @pl.when(has_next)
        def _():
            copy_prev(s).wait_recv()

        @pl.when(jnp.logical_not(has_prev))
        def _():
            for first, count in CHUNKS:
                own = [u_ref[c, pl.ds(first, count), :] for c in range(9)]
                outer = with_outer(None, own, ends_row(0), 0, -1.0)
                for c in range(9):
                    below[s, c, pl.ds(skip + first, count), :] = outer[c]

        @pl.when(jnp.logical_not(has_next))
        def _():
            for first, count in CHUNKS:
                own = [u_ref[c, pl.ds(top + first, count), :] for c in range(9)]
                outer = with_outer(None, own, ends_row(1), 0, 1.0)
                for c in range(9):
                    above[s, c, pl.ds(first, count), :] = outer[c]

        for first, count in CHUNKS:
            rows = pl.ds(first, count)
            left = [below[s, c, pl.ds(skip + first, count), :] for c in range(9)]
            flux = face_flux(left, [u_ref[c, rows, :] for c in range(9)], 0)
            for c in range(9):
                acc[c, rows, :] = acc[c, rows, :] + flux[c]
        for first, count in CHUNKS:
            rows = pl.ds(top + first, count)
            right = [above[s, c, pl.ds(first, count), :] for c in range(9)]
            flux = face_flux([u_ref[c, rows, :] for c in range(9)], right, 0)
            for c in range(9):
                acc[c, rows, :] = acc[c, rows, :] - flux[c]

    def update(s, step, spans):
        first, own, factor = STAGES[s]
        weight = step * factor
        for start, count in spans:
            for c in range(9):
                rows = pl.ds(start, count)
                new = own * states[s][c, rows, :] + weight * acc[c, rows, :]
                if first:
                    new = new + first * u0[c, rows, :]
                states[s + 1][c, rows, :] = new

    def peak_send_round(which):
        for step in range(1, rounds[which]):
            pltpu.make_async_remote_copy(
                src_ref=peak.at[which],
                dst_ref=peaks[which].at[step - 1],
                send_sem=peak_send.at[which],
                recv_sem=peak_recv.at[which],
                device_id=peer(which, step),
                device_id_type=MESH,
            ).start()

    def peak_wait_round(which):
        top = peak[which]
        if rounds[which] > 1:
            got = peaks[which]
            pltpu.make_async_copy(got, got, peak_recv.at[which]).wait()
            top = jnp.maximum(top, jnp.max(got[...], axis=0))
        peak[which + 1] = top

    inner_rows = ((HALO, NODES - 2 * HALO),)
    outer_rows = ((0, HALO), (NODES - HALO, HALO))

    def third_round():
        peak_wait_round(1)
        peak_send_round(2)

    load_u.wait()
    largest_speed()
    neighbours = sum(have.astype(jnp.int32) for have in (has_prev, has_next, has_left, has_right))
    pl.semaphore_wait(barrier, sum(rounds) - 3 + neighbours)
    peak_send_round(0)
    traces(u0, t_low, t_high)
    pack(t_low, own_low, 0, 0)
    pack(t_high, own_high, 0, wide - 1)
    send_width(0)
    for load in load_kinds:
        load.wait()
    low_wall = jnp.where(z == 0, wall_row(0), 3)
    high_wall = wall_row(1)

    step_row = None
    for s in range(3):
        if s:
            send_length(s)
        volume(s)
        if s == 0:
            peak_wait_round(0)
            peak_send_round(1)
            send_length(0)
            load_m.wait()
        derivatives(third_round if s == 0 else None)
        inner_faces(s, low_wall, high_wall)
        if s:
            update(s, step_row, inner_rows)
        length_edges(s)
        pack_width(s)
        if s < 2:
            send_width(s + 1)
        if s == 0:
            peak_wait_round(2)
            fastest = jnp.max(peak[3], axis=1, keepdims=True)
            step_row = CFL_NUMBER / (11.0 * jnp.broadcast_to(fastest, (1, LANES)))
            dt_ref[0, 0] = jnp.max(step_row)
            update(s, step_row, inner_rows)
        update(s, step_row, outer_rows)
        traces(states[s + 1], t_low, t_high)
        width_edges(s, step_row)
        scatter(s + 1)

    for which in range(3):
        if rounds[which] > 1:
            pltpu.make_async_copy(peaks[which], peaks[which], peak_send.at[which]).wait()
    for s in range(3):
        for have, copy in (
            (has_prev, copy_prev),
            (has_next, copy_next),
            (has_left, copy_left),
            (has_right, copy_right),
        ):

            @pl.when(have)
            def _(copy=copy):
                copy(s).wait_send()


def solution(mesh):
    nlen, nwid = mesh.shape["len"], mesh.shape["wid"]
    rounds = peak_rounds(nlen, nwid)
    matrix = volume_matrix()

    def on_device(conserved, ends_kind, sides_kind, walls_kind):
        f32 = jnp.float32
        vmem = pl.BlockSpec(memory_space=pltpu.VMEM)
        hbm = pl.BlockSpec(memory_space=pl.ANY)
        state = pltpu.VMEM((9, PADDED, LANES), f32)
        halo = pltpu.VMEM((3, 9, HALO, LANES), f32)
        pack = pltpu.VMEM((3, 9 * PACK, LANES), f32)
        own_pack = pltpu.VMEM((4, 9 * PACK, LANES), f32)
        trace = pltpu.VMEM((9, HALO, LANES), f32)
        flux = pltpu.VMEM((3 * PADDED, 9 * LANES), jnp.bfloat16)
        updated, step = pl.pallas_call(
            functools.partial(kernel, nlen, nwid),
            out_shape=(
                jax.ShapeDtypeStruct((9, NODES, LANES), f32),
                jax.ShapeDtypeStruct((1, 1), f32),
            ),
            in_specs=[hbm] * 5,
            out_specs=(vmem, pl.BlockSpec(memory_space=pltpu.SMEM)),
            scratch_shapes=[
                pltpu.VMEM((2, LANES // EZ, EZ), jnp.int32),
                pltpu.VMEM((2, 1, EZ), jnp.int32),
                pltpu.VMEM((2, 1, LANES // EZ), jnp.int32),
                state,
                state,
                state,
                pltpu.VMEM((2, PADDED, 3 * PADDED), jnp.bfloat16),
                flux,
                flux,
                state,
                halo,
                halo,
                own_pack,
                own_pack,
                pack,
                pack,
                pack,
                pack,
                pack,
                pack,
                pack,
                pack,
                trace,
                trace,
                trace,
                trace,
                trace,
                pltpu.VMEM((4, 1, LANES), f32),
                *(pltpu.VMEM((max(size - 1, 1), 1, LANES), f32) for size in rounds),
                pltpu.SemaphoreType.DMA((5,)),
                pltpu.SemaphoreType.DMA((3, 4)),
                pltpu.SemaphoreType.DMA((3, 4)),
                pltpu.SemaphoreType.DMA((3,)),
                pltpu.SemaphoreType.DMA((3,)),
            ],
            compiler_params=pltpu.CompilerParams(
                collective_id=0, has_side_effects=True, vmem_limit_bytes=40 * 1024 * 1024
            ),
        )(
            *(
                pltpu.with_memory_space_constraint(x, pltpu.HBM)
                for x in (
                    conserved.reshape(9, NODES, LANES),
                    jnp.asarray(matrix),
                    ends_kind,
                    sides_kind,
                    walls_kind,
                )
            )
        )
        return updated.reshape(conserved.shape), step.reshape(())

    return jax.shard_map(
        on_device,
        mesh=mesh,
        in_specs=(
            P(None, None, None, None, "len", "wid"),
            P(None, "wid", None),
            P(None, "len", None),
            P(None, "len", "wid"),
        ),
        out_specs=(P(None, None, None, None, "len", "wid"), P()),
        check_vma=False,
    )
```

```python
import functools

import jax
import jax.numpy as jnp
import numpy as np
from jax import lax
from jax.experimental import pallas as pl
from jax.experimental.pallas import tpu as pltpu
from jax.sharding import PartitionSpec as P

MESH = pl.DeviceIdType.MESH

EZ = 32
LANES = 128
NODES = 216
PADDED = 224
FACE = 36
HALO = 40
PACK = 9

GAMMA = 5.0 / 3.0
GLM_SPEED = 2.0
JET_SPEED = 0.8
BRAKE_FIELD = 1.0
CFL_NUMBER = 0.1
LIFT = 30.0

STAGES = ((0.0, 1.0, 1.0), (0.75, 0.25, 0.25), (1.0 / 3.0, 2.0 / 3.0, 2.0 / 3.0))


def lgl_derivative():
    points = np.array(
        [
            -1.0,
            -0.7650553239294647,
            -0.2852315164806451,
            0.2852315164806451,
            0.7650553239294647,
            1.0,
        ]
    )
    count = points.shape[0]
    barycentric = np.ones(count)
    for row in range(count):
        for column in range(count):
            if row != column:
                barycentric[row] = barycentric[row] / (points[row] - points[column])
    matrix = np.zeros((count, count))
    for row in range(count):
        for column in range(count):
            if row != column:
                matrix[row, column] = (
                    barycentric[column] / barycentric[row] / (points[row] - points[column])
                )
    for row in range(count):
        matrix[row, row] = -np.sum(matrix[row])
    return matrix.astype(np.float32)


def volume_matrix():
    line = lgl_derivative().astype(np.float64)
    line[0, 0] += LIFT / 2
    line[5, 5] -= LIFT / 2
    line = -2.0 * line
    eye = np.eye(6)
    whole = np.zeros((PADDED, 3 * PADDED))
    whole[:NODES, :NODES] = np.kron(np.kron(line, eye), eye)
    whole[:NODES, PADDED : PADDED + NODES] = np.kron(np.kron(eye, line), eye)
    whole[:NODES, 2 * PADDED : 2 * PADDED + NODES] = np.kron(np.kron(eye, eye), line)
    whole = whole.astype(np.float32)
    high = whole.astype(jnp.bfloat16)
    low = (whole - high.astype(np.float32)).astype(jnp.bfloat16)
    return np.stack([high, low])


def peak_rounds(nlen, nwid):
    near = min(8, nlen)
    return near, nwid // 2, nlen // near * 2


def root(x):
    return x * lax.rsqrt(jnp.maximum(x, 1e-30))


def primitives(u):
    inverse = 1.0 / u[0]
    velocity = [u[1] * inverse, u[2] * inverse, u[3] * inverse]
    kinetic = u[1] * velocity[0] + u[2] * velocity[1] + u[3] * velocity[2]
    squares = [u[5] * u[5], u[6] * u[6], u[7] * u[7]]
    field_sq = squares[0] + squares[1] + squares[2]
    pressure = (GAMMA - 1.0) * (u[4] - 0.5 * (kinetic + field_sq + u[8] * u[8]))
    return inverse, velocity, squares, field_sq, pressure


def fast_terms(prims):
    _, _, _, field_sq, pressure = prims
    acoustic = GAMMA * pressure
    gap = acoustic - field_sq
    return acoustic + field_sq, gap * gap, 4.0 * acoustic


def speed_along(prims, terms, d):
    inverse, velocity, squares, _, _ = prims
    both, gap_sq, acoustic4 = terms
    across = squares[(d + 1) % 3] + squares[(d + 2) % 3]
    inner = both + root(gap_sq + acoustic4 * across)
    return jnp.maximum(jnp.abs(velocity[d]) + root(0.5 * inverse * inner), GLM_SPEED)


def face_side(u, d):
    prims = primitives(u)
    _, velocity, _, field_sq, pressure = prims
    field = u[5:8]
    total = pressure + 0.5 * field_sq
    v, b = velocity[d], field[d]
    dot = velocity[0] * field[0] + velocity[1] * field[1] + velocity[2] * field[2]
    twice = GLM_SPEED * u[8]
    flux = [u[1 + d]]
    for c in range(3):
        entry = u[1 + c] * v - field[c] * b
        flux.append(entry + total if c == d else entry)
    flux.append(v * (u[4] + total) + b * (twice - dot))
    for c in range(3):
        flux.append(twice if c == d else v * field[c] - b * velocity[c])
    flux.append(GLM_SPEED * b)
    return flux, speed_along(prims, fast_terms(prims), d)


def face_flux(left, right, d):
    left_flux, left_speed = face_side(left, d)
    right_flux, right_speed = face_side(right, d)
    half = LIFT / 2
    largest = half * jnp.maximum(left_speed, right_speed)
    return [
        half * (left_flux[c] + right_flux[c]) - largest * (right[c] - left[c]) for c in range(9)
    ]


def inflow_value(c, d, outward):
    if c == 0:
        return 1.0
    if c == 1 + d:
        return -outward * JET_SPEED
    if c == 4:
        return 1.0 / (GAMMA - 1.0) + 0.5 * JET_SPEED**2 + 0.5 * BRAKE_FIELD**2
    if c == 7:
        return BRAKE_FIELD
    return 0.0


def with_outer(inner, interior, code, d, outward):
    states = []
    for c in range(9):
        x = interior[c]
        if c == 1 + d:
            x = jnp.where(code == 1, -x, x)
        x = jnp.where(code == 0, inflow_value(c, d, outward), x)
        states.append(x if inner is None else jnp.where(code < 3, x, inner[c]))
    return states


CHUNKS = ((0, 16), (16, 16), (32, 4))


def kernel(
    nlen,
    nwid,
    u_hbm,
    mat_hbm,
    ends_hbm,
    sides_hbm,
    walls_hbm,
    out_ref,
    dt_ref,
    ends_ref,
    sides_ref,
    walls_ref,
    u0,
    u1,
    u2,
    mat,
    fhi,
    flo,
    acc0,
    acc1,
    above,
    below,
    own_low,
    own_high,
    wide_below,
    wide_above,
    acc_low,
    acc_high,
    ghost_low,
    ghost_high,
    e_low,
    e_high,
    t_low,
    t_high,
    a_low,
    a_high,
    g_wide,
    peak,
    peaks0,
    peaks1,
    peaks2,
    load_sem,
    send_sem,
    recv_sem,
    peak_send,
    peak_recv,
):
    li = lax.axis_index("len")
    wi = lax.axis_index("wid")
    rounds = peak_rounds(nlen, nwid)
    near, rows_of_chips, columns = rounds
    lanes = lax.broadcasted_iota(jnp.int32, (1, LANES), 1)
    states = (u0, u1, u2, out_ref)
    accs = (acc0, acc1, acc1)
    peaks = (peaks0, peaks1, peaks2)

    load_u = pltpu.make_async_copy(u_hbm, u0.at[:, pl.ds(0, NODES), :], load_sem.at[0])
    load_m = pltpu.make_async_copy(mat_hbm, mat, load_sem.at[1])
    load_u.start()
    load_kinds = [
        pltpu.make_async_copy(src, dst, load_sem.at[2 + n])
        for n, (src, dst) in enumerate(
            ((ends_hbm, ends_ref), (sides_hbm, sides_ref), (walls_hbm, walls_ref))
        )
    ]
    for load in load_kinds:
        load.start()
    load_m.start()

    in_near, block = lax.rem(li, near), li // near
    in_column, row = lax.rem(wi, 2), wi // 2
    in_columns = block * 2 + in_column

    def peer(which, step):
        if which == 0:
            return (block * near + lax.rem(in_near + step, near), wi)
        if which == 1:
            return (li, lax.rem(row + step, rows_of_chips) * 2 + in_column)
        other = lax.rem(in_columns + step, columns)
        return ((other // 2) * near + in_near, row * 2 + lax.rem(other, 2))

    barrier = pltpu.get_barrier_semaphore()

    def greet(device):
        pl.semaphore_signal(barrier, inc=1, device_id=device, device_id_type=MESH)

    has_prev, has_next = li > 0, li < nlen - 1
    has_left, has_right = wi > 0, wi < nwid - 1

    for have, device in (
        (has_left, (li, wi - 1)),
        (has_right, (li, wi + 1)),
        (has_prev, (li - 1, wi)),
        (has_next, (li + 1, wi)),
    ):

        @pl.when(have)
        def _(device=device):
            greet(device)

    for which in (2, 1, 0):
        for step in range(1, rounds[which]):
            greet(peer(which, step))

    for ref in states[:3]:
        for c in range(9):
            ref[c, pl.ds(NODES, 8), :] = jnp.ones((8, LANES), jnp.float32)

    z = lanes % EZ
    y = lanes // EZ
    wide = LANES // EZ

    def tiled(row):
        return jnp.concatenate([row] * wide, axis=1)

    def wall_row(side):
        row = walls_ref[side]
        parts = [jnp.broadcast_to(row[:, q : q + 1], (1, EZ)) for q in range(wide)]
        return jnp.concatenate(parts, axis=1)

    def ends_row(side):
        return jnp.concatenate([ends_ref[side, q : q + 1, :] for q in range(wide)], axis=1)


    def copy_prev(s):
        return pltpu.make_async_remote_copy(
            src_ref=(u0, acc0, u2)[s].at[:, pl.ds(0, HALO), :],
            dst_ref=above.at[(0, 3, 2)[s]],
            send_sem=send_sem.at[s, 0],
            recv_sem=recv_sem.at[s, 0],
            device_id=(li - 1, wi),
            device_id_type=MESH,
        )

    def copy_next(s):
        return pltpu.make_async_remote_copy(
            src_ref=(u0, acc0, u2)[s].at[:, pl.ds(NODES - HALO, HALO), :],
            dst_ref=below.at[(0, 3, 2)[s]],
            send_sem=send_sem.at[s, 1],
            recv_sem=recv_sem.at[s, 1],
            device_id=(li + 1, wi),
            device_id_type=MESH,
        )

    def copy_left(s):
        return pltpu.make_async_remote_copy(
            src_ref=own_low.at[0] if s == 0 else acc_low.at[s - 1],
            dst_ref=wide_above.at[s],
            send_sem=send_sem.at[s, 2],
            recv_sem=recv_sem.at[s, 2],
            device_id=(li, wi - 1),
            device_id_type=MESH,
        )

    def copy_right(s):
        return pltpu.make_async_remote_copy(
            src_ref=own_high.at[0] if s == 0 else acc_high.at[s - 1],
            dst_ref=wide_below.at[s],
            send_sem=send_sem.at[s, 3],
            recv_sem=recv_sem.at[s, 3],
            device_id=(li, wi + 1),
            device_id_type=MESH,
        )

    def roll(x, by):
        by = by % LANES
        return x if by == 0 else pltpu.roll(x, by, axis=1)

    def packed(ref):
        return [ref[pl.ds(c, PACK, stride=9), :] for c in range(9)]

    def send_width(s):
        @pl.when(has_left)
        def _():
            copy_left(s).start()

        @pl.when(has_right)
        def _():
            copy_right(s).start()

    def send_length(s):
        @pl.when(has_prev)
        def _():
            copy_prev(s).start()

        @pl.when(has_next)
        def _():
            copy_next(s).start()

    def traces(ref, low, high):
        for c in range(9):
            for i in range(6):
                low[c, pl.ds(6 * i, 6), :] = ref[c, pl.ds(36 * i, 6), :]
                high[c, pl.ds(6 * i, 6), :] = ref[c, pl.ds(36 * i + 30, 6), :]

    def pack(ref, dest, slot, first):
        for c in range(9):
            whole = None
            for q in range(wide):
                piece = roll(ref[c, pl.ds(q, PACK, stride=4), :], EZ * (q - first))
                whole = piece if q == 0 else jnp.where(y == q, piece, whole)
            dest[slot, pl.ds(c, PACK, stride=9), :] = whole

    def pack_width(s):
        traces(accs[s], a_low, a_high)
        pack(a_low, acc_low, s, 0)
        pack(a_high, acc_high, s, wide - 1)

    def scatter(slot, low, high, target):
        for ref, src, first in ((low, own_low, 0), (high, own_high, wide - 1)):
            for c in range(9):
                new = src[slot, pl.ds(c, PACK, stride=9), :]
                for q in range(wide):
                    rows = pl.ds(q, PACK, stride=4)
                    ref[c, rows, :] = jnp.where(
                        y == first, roll(new, EZ * (first - q)), ref[c, rows, :]
                    )
        for c in range(9):
            for i in range(6):
                target[c, pl.ds(36 * i, 6), :] = low[c, pl.ds(6 * i, 6), :]
                target[c, pl.ds(36 * i + 30, 6), :] = high[c, pl.ds(6 * i, 6), :]

    def volume(s):
        u_ref = states[s]

        def put(d, c, parts):
            fhi[pl.ds(rows[d], 16), pl.ds(c * LANES, LANES)] = parts[0]
            flo[pl.ds(rows[d], 16), pl.ds(c * LANES, LANES)] = parts[1]

        def split(x):
            high = x.astype(jnp.bfloat16)
            return high, (x - high.astype(jnp.float32)).astype(jnp.bfloat16)

        rows = [None] * 3

        def body(chunk, _):
            start = pl.multiple_of(chunk * 16, 16)
            for d in range(3):
                rows[d] = pl.multiple_of(d * PADDED + chunk * 16, 16)
            u = [u_ref[c, pl.ds(start, 16), :] for c in range(9)]
            prims = primitives(u)
            _, velocity, _, field_sq, pressure = prims
            field = u[5:8]
            total = pressure + 0.5 * field_sq
            enthalpy = u[4] + total
            twice = GLM_SPEED * u[8]
            back = twice - (
                velocity[0] * field[0] + velocity[1] * field[1] + velocity[2] * field[2]
            )
            psi_parts = split(twice)
            for d in range(3):
                put(d, 0, split(u[1 + d]))
                put(d, 5 + d, psi_parts)
                put(d, 8, split(GLM_SPEED * field[d]))
                put(d, 4, split(velocity[d] * enthalpy + field[d] * back))
                put(d, 1 + d, split(u[1 + d] * velocity[d] - field[d] * field[d] + total))
                for e in range(d + 1, 3):
                    shear = split(u[1 + d] * velocity[e] - field[d] * field[e])
                    put(d, 1 + e, shear)
                    put(e, 1 + d, shear)
                    turn = split(velocity[d] * field[e] - field[d] * velocity[e])
                    put(d, 5 + e, turn)
                    put(e, 5 + d, (-turn[0], -turn[1]))
            return 0

        lax.fori_loop(0, PADDED // 16, body, 0)

    def largest_speed():
        def body(chunk, top):
            start = pl.multiple_of(chunk * 8, 8)
            prims = primitives([u0[c, pl.ds(start, 8), :] for c in range(9)])
            terms = fast_terms(prims)
            for d in range(3):
                top = jnp.maximum(top, speed_along(prims, terms, d))
            return top

        start = jnp.full((8, LANES), GLM_SPEED, jnp.float32)
        top = lax.fori_loop(0, NODES // 8, body, start, unroll=3)
        peak[0] = jnp.max(top, axis=0, keepdims=True)

    def derivatives(s, midway=None):
        acc = accs[s]
        for first in range(0, 9, 2):
            if first == 4 and midway is not None:
                midway()
            count = min(2, 9 - first)
            span = pl.ds(first * LANES, count * LANES)
            high = fhi[:, span]
            result = jnp.dot(mat[0], high, preferred_element_type=jnp.float32)
            result += jnp.dot(mat[1], high, preferred_element_type=jnp.float32)
            result += jnp.dot(mat[0], flo[:, span], preferred_element_type=jnp.float32)
            for c in range(count):
                acc[first + c] = result[:, c * LANES : (c + 1) * LANES]

    def inner_faces(s, low_wall, high_wall):
        acc = accs[s]
        u_ref = states[s]
        for first, count in CHUNKS:
            low_rows = pl.ds(6 * first, count, stride=6)
            high_rows = pl.ds(6 * first + 5, count, stride=6)
            low = [u_ref[c, low_rows, :] for c in range(9)]
            high = [u_ref[c, high_rows, :] for c in range(9)]
            beside = [roll(x, 1) for x in high]
            left = with_outer(beside, low, low_wall, 2, -1.0)
            flux = face_flux(left, low, 2)
            for c in range(9):
                acc[c, low_rows, :] = acc[c, low_rows, :] + flux[c]
            last = face_flux(high, with_outer(None, high, high_wall, 2, 1.0), 2)
            for c in range(9):
                upper = jnp.where(z == EZ - 1, last[c], roll(flux[c], -1))
                acc[c, high_rows, :] = acc[c, high_rows, :] - upper
        for first, count in CHUNKS:
            rows = pl.ds(first, count)
            low = [t_low[c, rows, :] for c in range(9)]
            left = [roll(t_high[c, rows, :], EZ) for c in range(9)]
            flux = face_flux(left, low, 1)
            for c in range(9):
                g_wide[c, rows, :] = flux[c]
        for c in range(9):
            for i in range(6):
                flux = g_wide[c, pl.ds(6 * i, 6), :]
                rows = pl.ds(36 * i, 6)
                acc[c, rows, :] = acc[c, rows, :] + jnp.where(y > 0, flux, 0.0)
                rows = pl.ds(36 * i + 30, 6)
                acc[c, rows, :] = acc[c, rows, :] - jnp.where(y < wide - 1, roll(flux, -EZ), 0.0)

    def advance(s, step, start, current, change):
        first, own, factor = STAGES[s]
        new = own * current + (step * factor) * change
        return new + first * start if first else new

    def width_edges(s, step):
        sides = (
            (has_left, copy_right, wide_below, ghost_low, e_low, -1.0, own_low, 0),
            (has_right, copy_left, wide_above, ghost_high, e_high, 1.0, own_high, 1),
        )
        for have, copy, received, ghost, edge, sign, own, side in sides:

            @pl.when(have)
            def _(copy=copy, received=received, ghost=ghost, edge=edge, sign=sign):
                copy(s).wait_recv()
                for c in range(9):
                    rows = pl.ds(c, PACK, stride=9)
                    new = received[s, rows, :]
                    if s:
                        change = new + sign * edge[s - 1, rows, :]
                        old = ghost[s - 1, rows, :]
                        new = advance(s - 1, step, ghost[0, rows, :], old, change)
                    ghost[s, rows, :] = new

            @pl.when(jnp.logical_not(have))
            def _(ghost=ghost, own=own, side=side, sign=sign):
                outer = with_outer(None, packed(own.at[s]), tiled(sides_ref[side]), 1, sign)
                for c in range(9):
                    ghost[s, pl.ds(c, PACK, stride=9), :] = outer[c]

        low = face_flux(packed(ghost_low.at[s]), packed(own_low.at[s]), 1)
        high = face_flux(packed(own_high.at[s]), packed(ghost_high.at[s]), 1)
        for fluxes, edge, own, change, sign in (
            (low, e_low, own_low, acc_low, 1.0),
            (high, e_high, own_high, acc_high, -1.0),
        ):
            for c in range(9):
                rows = pl.ds(c, PACK, stride=9)
                edge[s, rows, :] = fluxes[c]
                whole = change[s, rows, :] + sign * fluxes[c]
                if s != 1:
                    own[3, rows, :] = whole
                else:
                    own[s + 1, rows, :] = advance(
                        s, step, own[0, rows, :], own[s, rows, :], whole
                    )

    def first_width(step):
        for own in (own_low, own_high):
            for c in range(9):
                rows = pl.ds(c, PACK, stride=9)
                start = own[0, rows, :]
                own[1, rows, :] = advance(0, step, start, start, own[3, rows, :])

    def length_edges(s, step):
        u_ref = states[s]
        acc = accs[s]
        top = NODES - FACE
        skip = HALO - FACE

        @pl.when(has_prev)
        def _():
            copy_next(s).wait_recv()
            if s == 1:
                for c in range(9):
                    below[1, c] = advance(0, step, below[0, c], below[0, c], below[3, c])

        @pl.when(has_next)
        def _():
            copy_prev(s).wait_recv()
            if s == 1:
                for c in range(9):
                    above[1, c] = advance(0, step, above[0, c], above[0, c], above[3, c])

        @pl.when(jnp.logical_not(has_prev))
        def _():
            for first, count in CHUNKS:
                own = [u_ref[c, pl.ds(first, count), :] for c in range(9)]
                outer = with_outer(None, own, ends_row(0), 0, -1.0)
                for c in range(9):
                    below[s, c, pl.ds(skip + first, count), :] = outer[c]

        @pl.when(jnp.logical_not(has_next))
        def _():
            for first, count in CHUNKS:
                own = [u_ref[c, pl.ds(top + first, count), :] for c in range(9)]
                outer = with_outer(None, own, ends_row(1), 0, 1.0)
                for c in range(9):
                    above[s, c, pl.ds(first, count), :] = outer[c]

        for first, count in CHUNKS:
            rows = pl.ds(first, count)
            left = [below[s, c, pl.ds(skip + first, count), :] for c in range(9)]
            flux = face_flux(left, [u_ref[c, rows, :] for c in range(9)], 0)
            for c in range(9):
                acc[c, rows, :] = acc[c, rows, :] + flux[c]
        for first, count in CHUNKS:
            rows = pl.ds(top + first, count)
            right = [above[s, c, pl.ds(first, count), :] for c in range(9)]
            flux = face_flux([u_ref[c, rows, :] for c in range(9)], right, 0)
            for c in range(9):
                acc[c, rows, :] = acc[c, rows, :] - flux[c]

    def update(s, step, spans):
        first, own, factor = STAGES[s]
        weight = step * factor
        for start, count in spans:
            for c in range(9):
                rows = pl.ds(start, count)
                new = own * states[s][c, rows, :] + weight * accs[s][c, rows, :]
                if first:
                    new = new + first * u0[c, rows, :]
                states[s + 1][c, rows, :] = new

    def peak_send_round(which):
        for step in range(1, rounds[which]):
            pltpu.make_async_remote_copy(
                src_ref=peak.at[which],
                dst_ref=peaks[which].at[step - 1],
                send_sem=peak_send.at[which],
                recv_sem=peak_recv.at[which],
                device_id=peer(which, step),
                device_id_type=MESH,
            ).start()

    def peak_wait_round(which):
        top = peak[which]
        if rounds[which] > 1:
            got = peaks[which]
            pltpu.make_async_copy(got, got, peak_recv.at[which]).wait()
            top = jnp.maximum(top, jnp.max(got[...], axis=0))
        peak[which + 1] = top

    inner_rows = ((HALO, NODES - 2 * HALO),)
    outer_rows = ((0, HALO), (NODES - HALO, HALO))

    def third_round():
        peak_wait_round(1)
        peak_send_round(2)

    load_u.wait()
    largest_speed()
    neighbours = sum(have.astype(jnp.int32) for have in (has_prev, has_next, has_left, has_right))
    pl.semaphore_wait(barrier, sum(rounds) - 3 + neighbours)
    peak_send_round(0)
    traces(u0, t_low, t_high)
    pack(t_low, own_low, 0, 0)
    pack(t_high, own_high, 0, wide - 1)
    send_width(0)
    for load in load_kinds:
        load.wait()
    low_wall = jnp.where(z == 0, wall_row(0), 3)
    high_wall = wall_row(1)

    step_row = None
    for s in range(3):
        if s == 2:
            send_length(2)
        volume(s)
        if s == 0:
            peak_wait_round(0)
            peak_send_round(1)
            send_length(0)
            load_m.wait()
        derivatives(s, third_round if s == 0 else None)
        inner_faces(s, low_wall, high_wall)
        if s == 2:
            pack_width(2)
            width_edges(2, step_row)
            scatter(3, a_low, a_high, acc1)
            update(2, step_row, inner_rows)
            length_edges(2, step_row)
            update(2, step_row, outer_rows)
            break
        if s:
            update(s, step_row, inner_rows)
        length_edges(s, step_row)
        pack_width(s)
        send_width(s + 1)
        if s == 0:
            width_edges(0, None)
            scatter(3, a_low, a_high, acc0)
            send_length(1)
            peak_wait_round(2)
            fastest = jnp.max(peak[3], axis=1, keepdims=True)
            step_row = CFL_NUMBER / (11.0 * jnp.broadcast_to(fastest, (1, LANES)))
            dt_ref[0, 0] = jnp.max(step_row)
            update(0, step_row, inner_rows)
            update(0, step_row, outer_rows)
            traces(states[1], t_low, t_high)
            first_width(step_row)
        else:
            update(s, step_row, outer_rows)
            traces(states[s + 1], t_low, t_high)
            width_edges(s, step_row)
            scatter(s + 1, t_low, t_high, states[s + 1])

    for which in range(3):
        if rounds[which] > 1:
            pltpu.make_async_copy(peaks[which], peaks[which], peak_send.at[which]).wait()
    for s in range(3):
        for have, copy in (
            (has_prev, copy_prev),
            (has_next, copy_next),
            (has_left, copy_left),
            (has_right, copy_right),
        ):

            @pl.when(have)
            def _(copy=copy):
                copy(s).wait_send()


def solution(mesh):
    nlen, nwid = mesh.shape["len"], mesh.shape["wid"]
    rounds = peak_rounds(nlen, nwid)
    matrix = volume_matrix()

    def on_device(conserved, ends_kind, sides_kind, walls_kind):
        f32 = jnp.float32
        vmem = pl.BlockSpec(memory_space=pltpu.VMEM)
        hbm = pl.BlockSpec(memory_space=pl.ANY)
        state = pltpu.VMEM((9, PADDED, LANES), f32)
        halo = pltpu.VMEM((4, 9, HALO, LANES), f32)
        pack = pltpu.VMEM((3, 9 * PACK, LANES), f32)
        own_pack = pltpu.VMEM((4, 9 * PACK, LANES), f32)
        trace = pltpu.VMEM((9, HALO, LANES), f32)
        flux = pltpu.VMEM((3 * PADDED, 9 * LANES), jnp.bfloat16)
        updated, step = pl.pallas_call(
            functools.partial(kernel, nlen, nwid),
            out_shape=(
                jax.ShapeDtypeStruct((9, NODES, LANES), f32),
                jax.ShapeDtypeStruct((1, 1), f32),
            ),
            in_specs=[hbm] * 5,
            out_specs=(vmem, pl.BlockSpec(memory_space=pltpu.SMEM)),
            scratch_shapes=[
                pltpu.VMEM((2, LANES // EZ, EZ), jnp.int32),
                pltpu.VMEM((2, 1, EZ), jnp.int32),
                pltpu.VMEM((2, 1, LANES // EZ), jnp.int32),
                state,
                state,
                state,
                pltpu.VMEM((2, PADDED, 3 * PADDED), jnp.bfloat16),
                flux,
                flux,
                state,
                state,
                halo,
                halo,
                own_pack,
                own_pack,
                pack,
                pack,
                pack,
                pack,
                pack,
                pack,
                pack,
                pack,
                trace,
                trace,
                trace,
                trace,
                trace,
                pltpu.VMEM((4, 1, LANES), f32),
                *(pltpu.VMEM((max(size - 1, 1), 1, LANES), f32) for size in rounds),
                pltpu.SemaphoreType.DMA((5,)),
                pltpu.SemaphoreType.DMA((3, 4)),
                pltpu.SemaphoreType.DMA((3, 4)),
                pltpu.SemaphoreType.DMA((3,)),
                pltpu.SemaphoreType.DMA((3,)),
            ],
            compiler_params=pltpu.CompilerParams(
                collective_id=0, has_side_effects=True, vmem_limit_bytes=40 * 1024 * 1024
            ),
        )(
            *(
                pltpu.with_memory_space_constraint(x, pltpu.HBM)
                for x in (
                    conserved.reshape(9, NODES, LANES),
                    jnp.asarray(matrix),
                    ends_kind,
                    sides_kind,
                    walls_kind,
                )
            )
        )
        return updated.reshape(conserved.shape), step.reshape(())

    return jax.shard_map(
        on_device,
        mesh=mesh,
        in_specs=(
            P(None, None, None, None, "len", "wid"),
            P(None, "wid", None),
            P(None, "len", None),
            P(None, "len", "wid"),
        ),
        out_specs=(P(None, None, None, None, "len", "wid"), P()),
        check_vma=False,
    )
```

```python
import functools

import jax
import jax.numpy as jnp
import numpy as np
from jax import lax
from jax.experimental import pallas as pl
from jax.experimental.pallas import tpu as pltpu
from jax.sharding import PartitionSpec as P

MESH = pl.DeviceIdType.MESH

EZ = 32
LANES = 128
NODES = 216
PADDED = 224
FACE = 36
HALO = 40
PACK = 9

GAMMA = 5.0 / 3.0
GLM_SPEED = 2.0
JET_SPEED = 0.8
BRAKE_FIELD = 1.0
CFL_NUMBER = 0.1
LIFT = 30.0
ORDER = (1, 2, 0)

STAGES = ((0.0, 1.0, 1.0), (0.75, 0.25, 0.25), (1.0 / 3.0, 2.0 / 3.0, 2.0 / 3.0))


def lgl_derivative():
    points = np.array(
        [
            -1.0,
            -0.7650553239294647,
            -0.2852315164806451,
            0.2852315164806451,
            0.7650553239294647,
            1.0,
        ]
    )
    count = points.shape[0]
    barycentric = np.ones(count)
    for row in range(count):
        for column in range(count):
            if row != column:
                barycentric[row] = barycentric[row] / (points[row] - points[column])
    matrix = np.zeros((count, count))
    for row in range(count):
        for column in range(count):
            if row != column:
                matrix[row, column] = (
                    barycentric[column] / barycentric[row] / (points[row] - points[column])
                )
    for row in range(count):
        matrix[row, row] = -np.sum(matrix[row])
    return matrix.astype(np.float32)


def volume_matrix():
    line = lgl_derivative().astype(np.float64)
    line[0, 0] += LIFT / 2
    line[5, 5] -= LIFT / 2
    line = -2.0 * line
    eye = np.eye(6)
    whole = np.zeros((PADDED, 3 * PADDED))
    whole[:NODES, :NODES] = np.kron(np.kron(line, eye), eye)
    whole[:NODES, PADDED : PADDED + NODES] = np.kron(np.kron(eye, line), eye)
    whole[:NODES, 2 * PADDED : 2 * PADDED + NODES] = np.kron(np.kron(eye, eye), line)
    whole = whole.astype(np.float32)
    high = whole.astype(jnp.bfloat16)
    low = (whole - high.astype(np.float32)).astype(jnp.bfloat16)
    return np.stack([high, low])


def round_sizes(nlen, nwid):
    near = min(8, nlen)
    return near, nwid // 2, nlen // near * 2


def peak_rounds(nlen, nwid):
    return tuple(round_sizes(nlen, nwid)[n] for n in ORDER)


def root(x):
    return x * lax.rsqrt(jnp.maximum(x, 1e-30))


def primitives(u):
    inverse = 1.0 / u[0]
    velocity = [u[1] * inverse, u[2] * inverse, u[3] * inverse]
    kinetic = u[1] * velocity[0] + u[2] * velocity[1] + u[3] * velocity[2]
    squares = [u[5] * u[5], u[6] * u[6], u[7] * u[7]]
    field_sq = squares[0] + squares[1] + squares[2]
    pressure = (GAMMA - 1.0) * (u[4] - 0.5 * (kinetic + field_sq + u[8] * u[8]))
    return inverse, velocity, squares, field_sq, pressure


def fast_terms(prims):
    _, _, _, field_sq, pressure = prims
    acoustic = GAMMA * pressure
    gap = acoustic - field_sq
    return acoustic + field_sq, gap * gap, 4.0 * acoustic


def speed_along(prims, terms, d):
    inverse, velocity, squares, _, _ = prims
    both, gap_sq, acoustic4 = terms
    across = squares[(d + 1) % 3] + squares[(d + 2) % 3]
    inner = both + root(gap_sq + acoustic4 * across)
    return jnp.maximum(jnp.abs(velocity[d]) + root(0.5 * inverse * inner), GLM_SPEED)


def face_side(u, d):
    prims = primitives(u)
    _, velocity, _, field_sq, pressure = prims
    field = u[5:8]
    total = pressure + 0.5 * field_sq
    v, b = velocity[d], field[d]
    dot = velocity[0] * field[0] + velocity[1] * field[1] + velocity[2] * field[2]
    twice = GLM_SPEED * u[8]
    flux = [u[1 + d]]
    for c in range(3):
        entry = u[1 + c] * v - field[c] * b
        flux.append(entry + total if c == d else entry)
    flux.append(v * (u[4] + total) + b * (twice - dot))
    for c in range(3):
        flux.append(twice if c == d else v * field[c] - b * velocity[c])
    flux.append(GLM_SPEED * b)
    return flux, speed_along(prims, fast_terms(prims), d)


def face_flux(left, right, d):
    left_flux, left_speed = face_side(left, d)
    right_flux, right_speed = face_side(right, d)
    half = LIFT / 2
    largest = half * jnp.maximum(left_speed, right_speed)
    return [
        half * (left_flux[c] + right_flux[c]) - largest * (right[c] - left[c]) for c in range(9)
    ]


def inflow_value(c, d, outward):
    if c == 0:
        return 1.0
    if c == 1 + d:
        return -outward * JET_SPEED
    if c == 4:
        return 1.0 / (GAMMA - 1.0) + 0.5 * JET_SPEED**2 + 0.5 * BRAKE_FIELD**2
    if c == 7:
        return BRAKE_FIELD
    return 0.0


def with_outer(inner, interior, code, d, outward):
    states = []
    for c in range(9):
        x = interior[c]
        if c == 1 + d:
            x = jnp.where(code == 1, -x, x)
        x = jnp.where(code == 0, inflow_value(c, d, outward), x)
        states.append(x if inner is None else jnp.where(code < 3, x, inner[c]))
    return states


CHUNKS = ((0, 16), (16, 16), (32, 4))


def kernel(
    nlen,
    nwid,
    u_hbm,
    mat_hbm,
    ends_hbm,
    sides_hbm,
    walls_hbm,
    out_ref,
    dt_ref,
    ends_ref,
    sides_ref,
    walls_ref,
    u0,
    u1,
    u2,
    mat,
    fhi,
    flo,
    acc0,
    acc1,
    above,
    below,
    own_low,
    own_high,
    wide_below,
    wide_above,
    acc_low,
    acc_high,
    ghost_low,
    ghost_high,
    e_low,
    e_high,
    t_low,
    t_high,
    a_low,
    a_high,
    g_wide,
    peak,
    peaks0,
    peaks1,
    peaks2,
    load_sem,
    send_sem,
    recv_sem,
    peak_send,
    peak_recv,
):
    li = lax.axis_index("len")
    wi = lax.axis_index("wid")
    rounds = peak_rounds(nlen, nwid)
    near, rows_of_chips, columns = round_sizes(nlen, nwid)
    lanes = lax.broadcasted_iota(jnp.int32, (1, LANES), 1)
    states = (u0, u1, u2, out_ref)
    accs = (acc0, acc1, acc1)
    peaks = (peaks0, peaks1, peaks2)

    load_u = pltpu.make_async_copy(u_hbm, u0.at[:, pl.ds(0, NODES), :], load_sem.at[0])
    load_m = pltpu.make_async_copy(mat_hbm, mat, load_sem.at[1])
    load_u.start()
    load_kinds = [
        pltpu.make_async_copy(src, dst, load_sem.at[2 + n])
        for n, (src, dst) in enumerate(
            ((ends_hbm, ends_ref), (sides_hbm, sides_ref), (walls_hbm, walls_ref))
        )
    ]
    for load in load_kinds:
        load.start()
    load_m.start()

    in_near, block = lax.rem(li, near), li // near
    in_column, row = lax.rem(wi, 2), wi // 2
    in_columns = block * 2 + in_column

    def peer(which, step):
        which = ORDER[which]
        if which == 0:
            return (block * near + lax.rem(in_near + step, near), wi)
        if which == 1:
            return (li, lax.rem(row + step, rows_of_chips) * 2 + in_column)
        other = lax.rem(in_columns + step, columns)
        return ((other // 2) * near + in_near, row * 2 + lax.rem(other, 2))

    barrier = pltpu.get_barrier_semaphore()

    def greet(device):
        pl.semaphore_signal(barrier, inc=1, device_id=device, device_id_type=MESH)

    has_prev, has_next = li > 0, li < nlen - 1
    has_left, has_right = wi > 0, wi < nwid - 1

    for have, device in (
        (has_left, (li, wi - 1)),
        (has_right, (li, wi + 1)),
        (has_prev, (li - 1, wi)),
        (has_next, (li + 1, wi)),
    ):

        @pl.when(have)
        def _(device=device):
            greet(device)

    for which in (2, 1, 0):
        for step in range(1, rounds[which]):
            greet(peer(which, step))

    for ref in states[:3]:
        for c in range(9):
            ref[c, pl.ds(NODES, 8), :] = jnp.ones((8, LANES), jnp.float32)

    z = lanes % EZ
    y = lanes // EZ
    wide = LANES // EZ

    def tiled(row):
        return jnp.concatenate([row] * wide, axis=1)

    def wall_row(side):
        row = walls_ref[side]
        parts = [jnp.broadcast_to(row[:, q : q + 1], (1, EZ)) for q in range(wide)]
        return jnp.concatenate(parts, axis=1)

    def ends_row(side):
        return jnp.concatenate([ends_ref[side, q : q + 1, :] for q in range(wide)], axis=1)


    def copy_prev(s):
        return pltpu.make_async_remote_copy(
            src_ref=(u0, acc0, u2)[s].at[:, pl.ds(0, HALO), :],
            dst_ref=above.at[(0, 3, 2)[s]],
            send_sem=send_sem.at[s, 0],
            recv_sem=recv_sem.at[s, 0],
            device_id=(li - 1, wi),
            device_id_type=MESH,
        )

    def copy_next(s):
        return pltpu.make_async_remote_copy(
            src_ref=(u0, acc0, u2)[s].at[:, pl.ds(NODES - HALO, HALO), :],
            dst_ref=below.at[(0, 3, 2)[s]],
            send_sem=send_sem.at[s, 1],
            recv_sem=recv_sem.at[s, 1],
            device_id=(li + 1, wi),
            device_id_type=MESH,
        )

    def copy_left(s):
        return pltpu.make_async_remote_copy(
            src_ref=own_low.at[0] if s == 0 else acc_low.at[s - 1],
            dst_ref=wide_above.at[s],
            send_sem=send_sem.at[s, 2],
            recv_sem=recv_sem.at[s, 2],
            device_id=(li, wi - 1),
            device_id_type=MESH,
        )

    def copy_right(s):
        return pltpu.make_async_remote_copy(
            src_ref=own_high.at[0] if s == 0 else acc_high.at[s - 1],
            dst_ref=wide_below.at[s],
            send_sem=send_sem.at[s, 3],
            recv_sem=recv_sem.at[s, 3],
            device_id=(li, wi + 1),
            device_id_type=MESH,
        )

    def roll(x, by):
        by = by % LANES
        return x if by == 0 else pltpu.roll(x, by, axis=1)

    def packed(ref):
        return [ref[pl.ds(c, PACK, stride=9), :] for c in range(9)]

    def send_width(s):
        @pl.when(has_left)
        def _():
            copy_left(s).start()

        @pl.when(has_right)
        def _():
            copy_right(s).start()

    def send_length(s):
        @pl.when(has_prev)
        def _():
            copy_prev(s).start()

        @pl.when(has_next)
        def _():
            copy_next(s).start()

    def traces(ref, low, high):
        for c in range(9):
            for i in range(6):
                low[c, pl.ds(6 * i, 6), :] = ref[c, pl.ds(36 * i, 6), :]
                high[c, pl.ds(6 * i, 6), :] = ref[c, pl.ds(36 * i + 30, 6), :]

    def pack(ref, dest, slot, first):
        for c in range(9):
            whole = None
            for q in range(wide):
                piece = roll(ref[c, pl.ds(q, PACK, stride=4), :], EZ * (q - first))
                whole = piece if q == 0 else jnp.where(y == q, piece, whole)
            dest[slot, pl.ds(c, PACK, stride=9), :] = whole

    def pack_width(s):
        traces(accs[s], a_low, a_high)
        pack(a_low, acc_low, s, 0)
        pack(a_high, acc_high, s, wide - 1)

    def scatter(slot, low, high, target):
        for ref, src, first in ((low, own_low, 0), (high, own_high, wide - 1)):
            for c in range(9):
                new = src[slot, pl.ds(c, PACK, stride=9), :]
                for q in range(wide):
                    rows = pl.ds(q, PACK, stride=4)
                    ref[c, rows, :] = jnp.where(
                        y == first, roll(new, EZ * (first - q)), ref[c, rows, :]
                    )
        for c in range(9):
            for i in range(6):
                target[c, pl.ds(36 * i, 6), :] = low[c, pl.ds(6 * i, 6), :]
                target[c, pl.ds(36 * i + 30, 6), :] = high[c, pl.ds(6 * i, 6), :]

    def volume(s):
        u_ref = states[s]

        def put(d, c, parts):
            fhi[pl.ds(rows[d], 16), pl.ds(c * LANES, LANES)] = parts[0]
            flo[pl.ds(rows[d], 16), pl.ds(c * LANES, LANES)] = parts[1]

        def split(x):
            high = x.astype(jnp.bfloat16)
            return high, (x - high.astype(jnp.float32)).astype(jnp.bfloat16)

        rows = [None] * 3

        def body(chunk, _):
            start = pl.multiple_of(chunk * 16, 16)
            for d in range(3):
                rows[d] = pl.multiple_of(d * PADDED + chunk * 16, 16)
            u = [u_ref[c, pl.ds(start, 16), :] for c in range(9)]
            prims = primitives(u)
            _, velocity, _, field_sq, pressure = prims
            field = u[5:8]
            total = pressure + 0.5 * field_sq
            enthalpy = u[4] + total
            twice = GLM_SPEED * u[8]
            back = twice - (
                velocity[0] * field[0] + velocity[1] * field[1] + velocity[2] * field[2]
            )
            psi_parts = split(twice)
            for d in range(3):
                put(d, 0, split(u[1 + d]))
                put(d, 5 + d, psi_parts)
                put(d, 8, split(GLM_SPEED * field[d]))
                put(d, 4, split(velocity[d] * enthalpy + field[d] * back))
                put(d, 1 + d, split(u[1 + d] * velocity[d] - field[d] * field[d] + total))
                for e in range(d + 1, 3):
                    shear = split(u[1 + d] * velocity[e] - field[d] * field[e])
                    put(d, 1 + e, shear)
                    put(e, 1 + d, shear)
                    turn = split(velocity[d] * field[e] - field[d] * velocity[e])
                    put(d, 5 + e, turn)
                    put(e, 5 + d, (-turn[0], -turn[1]))
            return 0

        lax.fori_loop(0, PADDED // 16, body, 0)

    def largest_speed():
        def body(chunk, top):
            start = pl.multiple_of(chunk * 8, 8)
            prims = primitives([u0[c, pl.ds(start, 8), :] for c in range(9)])
            terms = fast_terms(prims)
            for d in range(3):
                top = jnp.maximum(top, speed_along(prims, terms, d))
            return top

        start = jnp.full((8, LANES), GLM_SPEED, jnp.float32)
        top = lax.fori_loop(0, NODES // 8, body, start, unroll=3)
        peak[0] = jnp.max(top, axis=0, keepdims=True)

    def derivatives(s, midway=None):
        acc = accs[s]
        for first in range(0, 9, 2):
            if first == 4 and midway is not None:
                midway()
            count = min(2, 9 - first)
            span = pl.ds(first * LANES, count * LANES)
            high = fhi[:, span]
            result = jnp.dot(mat[0], high, preferred_element_type=jnp.float32)
            result += jnp.dot(mat[1], high, preferred_element_type=jnp.float32)
            result += jnp.dot(mat[0], flo[:, span], preferred_element_type=jnp.float32)
            for c in range(count):
                acc[first + c] = result[:, c * LANES : (c + 1) * LANES]

    def inner_faces(s, low_wall, high_wall):
        acc = accs[s]
        u_ref = states[s]
        for first, count in CHUNKS:
            low_rows = pl.ds(6 * first, count, stride=6)
            high_rows = pl.ds(6 * first + 5, count, stride=6)
            low = [u_ref[c, low_rows, :] for c in range(9)]
            high = [u_ref[c, high_rows, :] for c in range(9)]
            beside = [roll(x, 1) for x in high]
            left = with_outer(beside, low, low_wall, 2, -1.0)
            flux = face_flux(left, low, 2)
            for c in range(9):
                acc[c, low_rows, :] = acc[c, low_rows, :] + flux[c]
            last = face_flux(high, with_outer(None, high, high_wall, 2, 1.0), 2)
            for c in range(9):
                upper = jnp.where(z == EZ - 1, last[c], roll(flux[c], -1))
                acc[c, high_rows, :] = acc[c, high_rows, :] - upper
        for first, count in CHUNKS:
            rows = pl.ds(first, count)
            low = [t_low[c, rows, :] for c in range(9)]
            left = [roll(t_high[c, rows, :], EZ) for c in range(9)]
            flux = face_flux(left, low, 1)
            for c in range(9):
                g_wide[c, rows, :] = flux[c]
        for c in range(9):
            for i in range(6):
                flux = g_wide[c, pl.ds(6 * i, 6), :]
                rows = pl.ds(36 * i, 6)
                acc[c, rows, :] = acc[c, rows, :] + jnp.where(y > 0, flux, 0.0)
                rows = pl.ds(36 * i + 30, 6)
                acc[c, rows, :] = acc[c, rows, :] - jnp.where(y < wide - 1, roll(flux, -EZ), 0.0)

    def advance(s, step, start, current, change):
        first, own, factor = STAGES[s]
        new = own * current + (step * factor) * change
        return new + first * start if first else new

    def width_edges(s, step):
        sides = (
            (has_left, copy_right, wide_below, ghost_low, e_low, -1.0, own_low, 0),
            (has_right, copy_left, wide_above, ghost_high, e_high, 1.0, own_high, 1),
        )
        for have, copy, received, ghost, edge, sign, own, side in sides:

            @pl.when(have)
            def _(copy=copy, received=received, ghost=ghost, edge=edge, sign=sign):
                copy(s).wait_recv()
                for c in range(9):
                    rows = pl.ds(c, PACK, stride=9)
                    new = received[s, rows, :]
                    if s:
                        change = new + sign * edge[s - 1, rows, :]
                        old = ghost[s - 1, rows, :]
                        new = advance(s - 1, step, ghost[0, rows, :], old, change)
                    ghost[s, rows, :] = new

            @pl.when(jnp.logical_not(have))
            def _(ghost=ghost, own=own, side=side, sign=sign):
                outer = with_outer(None, packed(own.at[s]), tiled(sides_ref[side]), 1, sign)
                for c in range(9):
                    ghost[s, pl.ds(c, PACK, stride=9), :] = outer[c]

        low = face_flux(packed(ghost_low.at[s]), packed(own_low.at[s]), 1)
        high = face_flux(packed(own_high.at[s]), packed(ghost_high.at[s]), 1)
        for fluxes, edge, own, change, sign in (
            (low, e_low, own_low, acc_low, 1.0),
            (high, e_high, own_high, acc_high, -1.0),
        ):
            for c in range(9):
                rows = pl.ds(c, PACK, stride=9)
                edge[s, rows, :] = fluxes[c]
                whole = change[s, rows, :] + sign * fluxes[c]
                if s != 1:
                    own[3, rows, :] = whole
                else:
                    own[s + 1, rows, :] = advance(
                        s, step, own[0, rows, :], own[s, rows, :], whole
                    )

    def first_width(step):
        for own in (own_low, own_high):
            for c in range(9):
                rows = pl.ds(c, PACK, stride=9)
                start = own[0, rows, :]
                own[1, rows, :] = advance(0, step, start, start, own[3, rows, :])

    def length_edges(s, step):
        u_ref = states[s]
        acc = accs[s]
        top = NODES - FACE
        skip = HALO - FACE

        @pl.when(has_prev)
        def _():
            copy_next(s).wait_recv()
            if s == 1:
                for c in range(9):
                    below[1, c] = advance(0, step, below[0, c], below[0, c], below[3, c])

        @pl.when(has_next)
        def _():
            copy_prev(s).wait_recv()
            if s == 1:
                for c in range(9):
                    above[1, c] = advance(0, step, above[0, c], above[0, c], above[3, c])

        @pl.when(jnp.logical_not(has_prev))
        def _():
            for first, count in CHUNKS:
                own = [u_ref[c, pl.ds(first, count), :] for c in range(9)]
                outer = with_outer(None, own, ends_row(0), 0, -1.0)
                for c in range(9):
                    below[s, c, pl.ds(skip + first, count), :] = outer[c]

        @pl.when(jnp.logical_not(has_next))
        def _():
            for first, count in CHUNKS:
                own = [u_ref[c, pl.ds(top + first, count), :] for c in range(9)]
                outer = with_outer(None, own, ends_row(1), 0, 1.0)
                for c in range(9):
                    above[s, c, pl.ds(first, count), :] = outer[c]

        for first, count in CHUNKS:
            rows = pl.ds(first, count)
            left = [below[s, c, pl.ds(skip + first, count), :] for c in range(9)]
            flux = face_flux(left, [u_ref[c, rows, :] for c in range(9)], 0)
            for c in range(9):
                acc[c, rows, :] = acc[c, rows, :] + flux[c]
        for first, count in CHUNKS:
            rows = pl.ds(top + first, count)
            right = [above[s, c, pl.ds(first, count), :] for c in range(9)]
            flux = face_flux([u_ref[c, rows, :] for c in range(9)], right, 0)
            for c in range(9):
                acc[c, rows, :] = acc[c, rows, :] - flux[c]

    def update(s, step, spans):
        first, own, factor = STAGES[s]
        weight = step * factor
        for start, count in spans:
            for c in range(9):
                rows = pl.ds(start, count)
                new = own * states[s][c, rows, :] + weight * accs[s][c, rows, :]
                if first:
                    new = new + first * u0[c, rows, :]
                states[s + 1][c, rows, :] = new

    def peak_send_round(which):
        for step in range(1, rounds[which]):
            pltpu.make_async_remote_copy(
                src_ref=peak.at[which],
                dst_ref=peaks[which].at[step - 1],
                send_sem=peak_send.at[which],
                recv_sem=peak_recv.at[which],
                device_id=peer(which, step),
                device_id_type=MESH,
            ).start()

    def peak_wait_round(which):
        top = peak[which]
        if rounds[which] > 1:
            got = peaks[which]
            pltpu.make_async_copy(got, got, peak_recv.at[which]).wait()
            top = jnp.maximum(top, jnp.max(got[...], axis=0))
        peak[which + 1] = top

    inner_rows = ((HALO, NODES - 2 * HALO),)
    outer_rows = ((0, HALO), (NODES - HALO, HALO))

    def third_round():
        peak_wait_round(1)
        peak_send_round(2)

    load_u.wait()
    largest_speed()
    neighbours = sum(have.astype(jnp.int32) for have in (has_prev, has_next, has_left, has_right))
    pl.semaphore_wait(barrier, sum(rounds) - 3 + neighbours)
    peak_send_round(0)
    traces(u0, t_low, t_high)
    pack(t_low, own_low, 0, 0)
    pack(t_high, own_high, 0, wide - 1)
    send_width(0)
    for load in load_kinds:
        load.wait()
    low_wall = jnp.where(z == 0, wall_row(0), 3)
    high_wall = wall_row(1)

    step_row = None
    for s in range(3):
        if s == 2:
            send_length(2)
        volume(s)
        if s == 0:
            peak_wait_round(0)
            peak_send_round(1)
            send_length(0)
            load_m.wait()
        derivatives(s, third_round if s == 0 else None)
        inner_faces(s, low_wall, high_wall)
        if s == 2:
            pack_width(2)
            width_edges(2, step_row)
            scatter(3, a_low, a_high, acc1)
            update(2, step_row, inner_rows)
            length_edges(2, step_row)
            update(2, step_row, outer_rows)
            break
        if s:
            update(s, step_row, inner_rows)
        length_edges(s, step_row)
        pack_width(s)
        send_width(s + 1)
        if s == 0:
            width_edges(0, None)
            scatter(3, a_low, a_high, acc0)
            send_length(1)
            peak_wait_round(2)
            fastest = jnp.max(peak[3], axis=1, keepdims=True)
            step_row = CFL_NUMBER / (11.0 * jnp.broadcast_to(fastest, (1, LANES)))
            dt_ref[0, 0] = jnp.max(step_row)
            update(0, step_row, inner_rows)
            update(0, step_row, outer_rows)
            traces(states[1], t_low, t_high)
            first_width(step_row)
        else:
            update(s, step_row, outer_rows)
            traces(states[s + 1], t_low, t_high)
            width_edges(s, step_row)
            scatter(s + 1, t_low, t_high, states[s + 1])

    for which in range(3):
        if rounds[which] > 1:
            pltpu.make_async_copy(peaks[which], peaks[which], peak_send.at[which]).wait()
    for s in range(3):
        for have, copy in (
            (has_prev, copy_prev),
            (has_next, copy_next),
            (has_left, copy_left),
            (has_right, copy_right),
        ):

            @pl.when(have)
            def _(copy=copy):
                copy(s).wait_send()


def solution(mesh):
    nlen, nwid = mesh.shape["len"], mesh.shape["wid"]
    rounds = peak_rounds(nlen, nwid)
    matrix = volume_matrix()

    def on_device(conserved, ends_kind, sides_kind, walls_kind):
        f32 = jnp.float32
        vmem = pl.BlockSpec(memory_space=pltpu.VMEM)
        hbm = pl.BlockSpec(memory_space=pl.ANY)
        state = pltpu.VMEM((9, PADDED, LANES), f32)
        halo = pltpu.VMEM((4, 9, HALO, LANES), f32)
        pack = pltpu.VMEM((3, 9 * PACK, LANES), f32)
        own_pack = pltpu.VMEM((4, 9 * PACK, LANES), f32)
        trace = pltpu.VMEM((9, HALO, LANES), f32)
        flux = pltpu.VMEM((3 * PADDED, 9 * LANES), jnp.bfloat16)
        updated, step = pl.pallas_call(
            functools.partial(kernel, nlen, nwid),
            out_shape=(
                jax.ShapeDtypeStruct((9, NODES, LANES), f32),
                jax.ShapeDtypeStruct((1, 1), f32),
            ),
            in_specs=[hbm] * 5,
            out_specs=(vmem, pl.BlockSpec(memory_space=pltpu.SMEM)),
            scratch_shapes=[
                pltpu.VMEM((2, LANES // EZ, EZ), jnp.int32),
                pltpu.VMEM((2, 1, EZ), jnp.int32),
                pltpu.VMEM((2, 1, LANES // EZ), jnp.int32),
                state,
                state,
                state,
                pltpu.VMEM((2, PADDED, 3 * PADDED), jnp.bfloat16),
                flux,
                flux,
                state,
                state,
                halo,
                halo,
                own_pack,
                own_pack,
                pack,
                pack,
                pack,
                pack,
                pack,
                pack,
                pack,
                pack,
                trace,
                trace,
                trace,
                trace,
                trace,
                pltpu.VMEM((4, 1, LANES), f32),
                *(pltpu.VMEM((max(size - 1, 1), 1, LANES), f32) for size in rounds),
                pltpu.SemaphoreType.DMA((5,)),
                pltpu.SemaphoreType.DMA((3, 4)),
                pltpu.SemaphoreType.DMA((3, 4)),
                pltpu.SemaphoreType.DMA((3,)),
                pltpu.SemaphoreType.DMA((3,)),
            ],
            compiler_params=pltpu.CompilerParams(
                collective_id=0, has_side_effects=True, vmem_limit_bytes=40 * 1024 * 1024
            ),
        )(
            *(
                pltpu.with_memory_space_constraint(x, pltpu.HBM)
                for x in (
                    conserved.reshape(9, NODES, LANES),
                    jnp.asarray(matrix),
                    ends_kind,
                    sides_kind,
                    walls_kind,
                )
            )
        )
        return updated.reshape(conserved.shape), step.reshape(())

    return jax.shard_map(
        on_device,
        mesh=mesh,
        in_specs=(
            P(None, None, None, None, "len", "wid"),
            P(None, "wid", None),
            P(None, "len", None),
            P(None, "len", "wid"),
        ),
        out_specs=(P(None, None, None, None, "len", "wid"), P()),
        check_vma=False,
    )
```
